32 devices in a mesh: slab: 8 (over z, y), batch: 4 (over x, core).
Axes of the slice: x: 2, y: 2, z: 4, core: 2. Of those that a mesh axis runs over, the one named last changes fastest.
Arguments:
- velocity_old: float32 [64, 64, 2, 3, 128], P('slab', 'batch'), may hold values from -6 to 6
- traction: bfloat16 [6144, 3, 169], P(('slab', 'batch')), may hold values from -6 to 6
- offsets: bfloat16 [6144, 3, 338], P(('slab', 'batch')), may hold values from -1 to 2
- owner_slab: int32 [6144, 1], P(('slab', 'batch')), may hold values from 0 to 7; in each aligned block of 192 rows (0 to 191, 192 to 383, ...) at most 48 rows name the same one
- anchor: int32 [6144, 3], P(('slab', 'batch')), may hold values from 1 to 253, as said below
- blocks: int32 [6144, 16], P(('slab', 'batch')), may hold values from 0 to 1023, as said below
- block_count: int32 [6144], P(('slab', 'batch')), may hold values from 8 to 16, as said below
- synthesis: bfloat16 [169, 338], replicated, may hold values from -0.5 to 0.5
- analysis: bfloat16 [169, 338], replicated, may hold values from -0.3125 to 0.3125
Outputs:
- velocity_new: float32 [64, 64, 2, 3, 128], P('slab', 'batch')
- velocity_coef: bfloat16 [6144, 3, 169], P(('slab', 'batch'))
The draws below stay inside these ranges and needn't reach their ends.
Inputs may be any that keep to these rules, and one draw needn't show every extreme that they name: `owner_slab`: among the 192 cells of one device at most 48 name the same slab, and that bound is reached. `anchor`: in the owner's slab: first coordinate 1 to 5, second 1 to 61, third 1 to 125 within its tile of 128 points. `blocks`: the first block_count entries of a cell are distinct lines within two cells of its anchor in the first two dimensions, in its anchor's tile along the third; the remaining entries are padding with any tile number. `block_count`: some cells of every device use all 16 blocks.
All inputs are finite; a program needn't handle non-finite values.
Results may differ from the reference program's by a relative error of at most 0.012.
Values may be sent and summed in bfloat16 or wider, within the bound.
No kernel may reach another device: no remote copies, remote signals or barrier semaphores. Data moves between devices by JAX's collectives and lax.ppermute only.
A program may use at most 64 MiB of HBM per device.

```python
import math
import jax
import jax.numpy as jnp
import numpy as np
from jax import lax

L = 169
Q = 338
B = 16
SWEEPS = 2
GX = 8
NY = 64
NZ = 256
CELLS_DEV = 192
CAP = 48
NX = 64
CELLS = 6144
N_SLAB = 8


def stencil_layout(key):
    base = jax.random.fold_in(key, 11)
    subkeys = jax.random.split(base, 7)
    layers = NZ // 128
    tiles_dev = GX * NY * layers
    anchor_x = jax.random.randint(subkeys[0], (CELLS,), 1, GX - 2)
    anchor_y = jax.random.randint(subkeys[1], (CELLS,), 1, NY - 2)
    tile_z = jax.random.randint(subkeys[2], (CELLS,), 0, layers)
    anchor_z = tile_z * 128 + jax.random.randint(subkeys[3], (CELLS,), 1, 126)
    line_index = jnp.arange(16)
    shift_x = line_index // 4 - 1
    shift_y = line_index % 4 - 1
    scores = jax.random.randint(subkeys[4], (CELLS, 16), 0, 4096) * 16 + line_index[None, :]
    chosen = jnp.argsort(scores, axis=1)[:, :B]
    tile_ids = ((anchor_x[:, None] + shift_x[chosen]) * NY + anchor_y[:, None] + shift_y[chosen]) * layers + tile_z[:, None]
    drawn_count = jax.random.randint(subkeys[5], (CELLS,), B // 2, B + 1)
    pinned = jnp.arange(CELLS) % 4 == 0
    count = jnp.where(pinned, B, drawn_count)
    filler = jax.random.randint(subkeys[6], (CELLS, B), 0, tiles_dev)
    blocks = jnp.where(jnp.arange(B)[None, :] < count[:, None], tile_ids, filler)
    anchor = jnp.stack([anchor_x, anchor_y, anchor_z], axis=1)
    return (anchor.astype(jnp.int32), blocks.astype(jnp.int32), count.astype(jnp.int32))


def draw_anchor(key, part):
    return stencil_layout(key)[0]


def draw_blocks(key, part):
    return stencil_layout(key)[1]


def draw_block_count(key, part):
    return stencil_layout(key)[2]


def block_levels(own_key, extent, shards, least, high):
    def one(axis_at, shards_of):
        steps = jax.random.uniform(jax.random.fold_in(jax.random.fold_in(own_key, 6), axis_at), (shards_of,), jnp.float32, least / len(shards), high / len(shards))
        return jnp.repeat(jnp.exp(steps), extent[axis_at] // shards_of).reshape((-1,) + (1,) * (len(extent) - axis_at - 1))

    gain = one(*shards[0])
    for cut in shards[1:]:
        gain = gain * one(*cut)
    return gain


def routed_block(rng, own, number, rows, count, top, most, slope):
    sequence = jax.random.permutation(rng, count)
    heavy_load, usual = load_shares(count, rows * top, most, slope, True), load_shares(count, rows * top, most, slope, False)
    places = jnp.arange(count)

    def named(tallies, turn):
        used = int((tallies > 0).sum())
        fixed = max(1, used // 4)
        shifted = fixed + (places - fixed + turn * (used - fixed)) % max(1, count - fixed)
        return jnp.zeros((count,), jnp.int32).at[sequence[jnp.where(places < fixed, places, shifted)]].set(jnp.asarray(tallies, jnp.int32))

    tallies = jnp.where(number % 4 == 0, named(heavy_load, number // 4), named(usual, number - number // 4 - 1))
    mixed = jax.random.permutation(jax.random.fold_in(own, 3), count)
    giver, taker = mixed[0:count // 2 * 2:2], mixed[1:count // 2 * 2:2]
    room = jnp.minimum(tallies[giver] - 1, most - tallies[taker]) // 2
    room = jnp.where((giver == sequence[0]) | (taker == sequence[0]) | (tallies[taker] == 0), 0, jnp.maximum(room, 0))
    shifted = jax.random.randint(jax.random.fold_in(own, 4), (count // 2,), 0, 1 << 20) % (room + 1)
    tallies = tallies.at[giver].add(-shifted).at[taker].add(shifted)
    members = jnp.searchsorted(jnp.cumsum(tallies), jnp.arange(rows * top), side="right").astype(jnp.int32)
    table = members.reshape(top, rows).T
    table = table[jax.random.permutation(jax.random.fold_in(own, 1), rows)]
    turn = jax.random.randint(jax.random.fold_in(own, 2), (rows, 1), 0, top)
    return jnp.take_along_axis(table, (jnp.arange(top)[None, :] + turn) % top, axis=1)


def load_shares(count, total, bound, lean, full):
    portions = [(1 << 20) // math.isqrt(grade ** lean) + 1 for grade in range(1, count + 1)]
    largest = bound if full else min(bound, max(-(-total // count), total * portions[0] // sum(portions)))
    least = 1 if total - largest >= count - 1 else 0
    given, rest = [largest] + [least] * (count - 1), total - largest - least * (count - 1)
    while rest > 0:
        movable = [i for i in range(1, count) if given[i] < largest] or [i for i in range(1, count) if given[i] < bound]
        whole, budget = sum([portions[i] for i in movable]), rest
        for i in movable:
            more = min(bound - given[i], max(1, budget * portions[i] // whole), rest)
            given[i] = given[i] + more
            rest = rest - more
    return np.array(given)


def centred(own_key, shape, scale, most, cuts=(), kind=jnp.bfloat16):
    level = block_levels(own_key, shape, cuts, -0.22, 0.18) if cuts else 1.0
    values = jax.random.normal(own_key, shape, jnp.float32) * scale * level
    return jnp.minimum(jnp.maximum(values, -most), most).astype(kind)


def setup_inputs(seed: int = 0) -> dict:
    arg_keys = jax.random.split(jax.random.key(seed), 10)
    velocity_old = centred(arg_keys[0], (NX, NY, NZ // 128, 3, 128), 1.0, 6.0, ((0, 8), (1, 4)), jnp.float32)
    traction = centred(arg_keys[1], (CELLS, 3, L), 1.0, 6.0, ((0, 32),))
    offsets = jnp.clip(-1.0 + 3.0 * jax.random.uniform(arg_keys[2], (CELLS, 3, Q), jnp.float32) ** block_levels(arg_keys[2], (CELLS, 3, Q), ((0, 32),), -0.2, 0.2), -1.0, 2.0).astype(jnp.bfloat16)
    owner_slab_keys = jax.random.split(jax.random.fold_in(arg_keys[3], 1), CELLS // CELLS_DEV)
    owner_slab_turns = jax.random.permutation(jax.random.fold_in(arg_keys[3], 3), CELLS // CELLS_DEV)
    owner_slab = jax.vmap(lambda own, number: routed_block(jax.random.fold_in(arg_keys[3], 2), own, number, CELLS_DEV, N_SLAB, 1, CAP, 2))(owner_slab_keys, owner_slab_turns).reshape((CELLS, 1))
    anchor = draw_anchor(jax.random.fold_in(arg_keys[9], 71), 0)
    blocks = draw_blocks(jax.random.fold_in(arg_keys[9], 71), 0)
    block_count = draw_block_count(jax.random.fold_in(arg_keys[9], 71), 0)
    synthesis = centred(arg_keys[7], (L, Q), L ** -0.5, 0.5)
    analysis = centred(arg_keys[8], (L, Q), Q ** -0.5, 0.3125)
    return {"velocity_old": velocity_old, "traction": traction, "offsets": offsets, "owner_slab": owner_slab, "anchor": anchor, "blocks": blocks, "block_count": block_count, "synthesis": synthesis, "analysis": analysis}


kernel_width = 0.8
kernel_norm = 1.0 / (0.8 * math.sqrt(2.0 * math.pi))
coupling = 2.0

def kernel_value(distance):
    scaled = distance / kernel_width
    return jnp.exp(-0.5 * scaled * scaled) * kernel_norm

def stencil_weights(anchor_part, offset_part, block_part, count_part):
    layers = NZ // 128
    points = anchor_part[:, :, None].astype(jnp.float32) + offset_part.astype(jnp.float32)
    tile_x = (block_part // (NY * layers)).astype(jnp.float32)
    tile_y = (block_part // layers % NY).astype(jnp.float32)
    live_mask = (jnp.arange(block_part.shape[1])[None, :] < count_part[:, None]).astype(jnp.float32)
    weight_xy = kernel_value(points[:, 0, None, :] - tile_x[:, :, None]) * kernel_value(points[:, 1, None, :] - tile_y[:, :, None]) * live_mask[:, :, None]
    z_root = (anchor_part[:, 2] // 128 * 128).astype(jnp.float32)
    heights = z_root[:, None, None] + jnp.arange(128, dtype=jnp.float32)[None, None, :]
    weight_z = kernel_value(points[:, 2, :, None] - heights).astype(jnp.bfloat16)
    return (weight_xy, weight_z)

def neighbours(padded):
    centre = padded[1:-1, 1:-1]
    total = padded[2:, 1:-1] + padded[:-2, 1:-1] + padded[1:-1, 2:] + padded[1:-1, :-2]
    zero_edge = jnp.zeros(centre.shape[:2] + (1, centre.shape[3], 1), centre.dtype)
    after = jnp.concatenate([centre[:, :, 1:, :, :1], zero_edge], axis=2)
    before = jnp.concatenate([zero_edge, centre[:, :, :-1, :, -1:]], axis=2)
    upper = jnp.concatenate([centre[..., 1:], after], axis=-1)
    lower = jnp.concatenate([before, centre[..., :-1]], axis=-1)
    return total + upper + lower

def relax(drive, widen):
    state = drive
    for sweep_index in range(SWEEPS):
        state = (drive + coupling * neighbours(widen(state))) / (1.0 + 6.0 * coupling)
    return state

def reference(velocity_old, traction, offsets, owner_slab, anchor, blocks, block_count, synthesis, analysis):
    layers = NZ // 128
    tiles_dev = GX * NY * layers
    groups = CELLS // CELLS_DEV

    def split_cells(values):
        return values.reshape((groups, CELLS_DEV) + values.shape[1:])
    cell_data = tuple((split_cells(values) for values in (traction, offsets, owner_slab[:, 0], anchor, blocks, block_count)))

    def spread_step(grid_sum, piece):
        coef_part, offset_part, owner_part, anchor_part, block_part, count_part = piece
        weight_xy, weight_z = stencil_weights(anchor_part, offset_part, block_part, count_part)
        forces = jnp.einsum('ckl,lq->ckq', coef_part.astype(jnp.float32), synthesis.astype(jnp.float32))
        weighted = (forces[:, None] * weight_xy[:, :, None]).astype(jnp.bfloat16)
        tile_terms = jnp.einsum('cbkq,cqi->cbki', weighted.astype(jnp.float32), weight_z.astype(jnp.float32))
        targets = (owner_part[:, None] * tiles_dev + block_part).reshape(-1)
        return (grid_sum.at[targets].add(tile_terms.reshape(-1, 3, 128)), None)
    start = jnp.zeros((NX * NY * layers, 3, 128), jnp.float32)
    forcing, ignored = lax.scan(spread_step, start, cell_data)
    drive = velocity_old + forcing.reshape(velocity_old.shape)

    def widen(state):
        return jnp.pad(state, ((1, 1), (1, 1), (0, 0), (0, 0), (0, 0)))
    velocity_new = relax(drive, widen)
    flat_velocity = velocity_new.astype(jnp.bfloat16).reshape(-1, 3, 128)

    def sample_step(piece):
        coef_part, offset_part, owner_part, anchor_part, block_part, count_part = piece
        weight_xy, weight_z = stencil_weights(anchor_part, offset_part, block_part, count_part)
        targets = owner_part[:, None] * tiles_dev + block_part
        gathered = flat_velocity[targets]
        projected = jnp.einsum('cbki,cqi->cbkq', gathered.astype(jnp.float32), weight_z.astype(jnp.float32))
        point_velocity = lax.optimization_barrier(jnp.sum(projected * weight_xy[:, :, None, :], axis=1)).astype(jnp.bfloat16)
        return jnp.einsum('ckq,lq->ckl', point_velocity.astype(jnp.float32), analysis.astype(jnp.float32)).astype(jnp.bfloat16)
    coefs = lax.map(sample_step, cell_data)
    return (velocity_new, coefs.reshape(CELLS, 3, analysis.shape[0]))
```

```python
import math

import jax
import jax.numpy as jnp
from jax import lax
from jax.experimental import pallas as pl
from jax.experimental.pallas import tpu as pltpu
from jax.sharding import PartitionSpec as P

SWEEPS = 2
TILE = 128
GROUP = 8
DEAD = 64.0

kernel_width = 0.8
kernel_norm = 1.0 / (0.8 * math.sqrt(2.0 * math.pi))
coupling = 2.0
scale = math.sqrt(0.5 / math.log(2.0)) / kernel_width
norm_bits = math.log2(kernel_norm)

f32 = jnp.float32
bf16 = jnp.bfloat16


def round_up(value, step):
    return -(-value // step) * step


def iota(shape, dim):
    return lax.broadcasted_iota(jnp.int32, shape, dim)


def one_hot(mask):
    return jnp.where(mask, 1.0, 0.0).astype(bf16)


def dot(a, b, ca=1, cb=0):
    return lax.dot_general(a, b, (((ca,), (cb,)), ((), ())), preferred_element_type=f32)


def vmem(count=1):
    return [pl.BlockSpec(memory_space=pltpu.VMEM)] * count


def smem(count=1):
    return [pl.BlockSpec(memory_space=pltpu.SMEM)] * count


params = pltpu.CompilerParams(vmem_limit_bytes=48 * 1024 * 1024)


class Sizes:
    def __init__(self, terms, points, stencil):
        self.terms, self.points, self.stencil = terms, points, stencil
        self.qw = round_up(points, TILE)
        self.cw = round_up(3 * terms, TILE)
        self.width = 3 * self.qw + self.cw
        self.mt = points // TILE * TILE
        self.mo = points - self.mt
        self.meta = 2 * stencil + 4
        self.rows = round_up(self.meta, 8)


def place_terms(sz, k):
    shape = (sz.cw, sz.terms)
    return one_hot(iota(shape, 0) == iota(shape, 1) + k * sz.terms)


def pack_kernel(sz, slabs, cap, ny, layers, owner, anchor, blocks, count, trac, offs, send, slot_out, rec):
    cells = owner.shape[1]
    slots = slabs * cap
    own = owner[...]
    member = one_hot(own == iota((slabs, cells), 0))
    before = one_hot(iota((cells, cells), 0) < iota((cells, cells), 1))
    rank = jnp.sum(member.astype(f32) * dot(member, before), axis=0, keepdims=True)
    slot = own * cap + rank.astype(jnp.int32)
    slot_out[...] = slot
    place = one_hot(slot == iota((slots, cells), 0))

    tile = blocks[...].astype(f32)
    anchors = anchor[...].astype(f32)
    tile_x = jnp.floor((tile + 0.5) * (1.0 / (ny * layers)))
    tile_y = jnp.floor((tile + 0.5) * (1.0 / layers)) - tile_x * ny
    live = iota(tile.shape, 0) < count[...]
    dx = jnp.where(live, tile_x - anchors[0:1], DEAD)
    dy = jnp.where(live, tile_y - anchors[1:2], DEAD)

    rec[...] = jnp.zeros(rec.shape, bf16)
    for k in range(3):
        rec[:, k * sz.qw : k * sz.qw + sz.points] = offs[k]
    base = sz.mo
    meta = jnp.zeros((cells, TILE), f32)
    ones = jnp.ones((1, cells), f32)
    for part in (dx, dy, anchors, ones):
        shape = (part.shape[0], TILE)
        where = one_hot(iota(shape, 1) == iota(shape, 0) + base)
        meta = meta + dot(part.astype(bf16), where, 0, 0)
        base += part.shape[0]
    rec[:, sz.mt : sz.mt + TILE] = rec[:, sz.mt : sz.mt + TILE] + meta.astype(bf16)
    coef = jnp.zeros((cells, sz.cw), f32)
    for k in range(3):
        coef = coef + dot(trac[k], place_terms(sz, k), 0, 1)
    rec[:, 3 * sz.qw :] = coef.astype(bf16)
    send[...] = dot(place, rec[...]).astype(bf16)


def meta_table(sz, recv):
    shape = (sz.rows, TILE)
    pick = one_hot((iota(shape, 1) == iota(shape, 0) + sz.mo) & (iota(shape, 0) < sz.meta))
    return dot(pick, recv[:, sz.mt : sz.mt + TILE], 1, 1)


def height_weights(pz_row):
    heights = iota((TILE, TILE), 0).astype(f32) * scale
    away = jnp.broadcast_to(pz_row, (TILE, TILE)) - heights
    return jnp.exp2(norm_bits - away * away).astype(bf16)


def line_weights(ox_row, oy_row, dx, dy):
    ex = ox_row - dx
    ey = oy_row - dy
    return jnp.exp2(2.0 * norm_bits - ex * ex - ey * ey)


def column_group(sz, cols, g):
    per = TILE // GROUP
    wide = cols[g // per]
    return pltpu.roll(wide, (TILE - GROUP * (g % per)) % TILE, 1)


def spread_kernel(
    sz, gx, ny, nyb, layers, where, recv, synthesis, vold,
    keep, send, points, cols, rows_out,
    grid, forces, expand, terms, rows_v, rows_s, sem,
):
    slots = recv.shape[0]
    planes = 3 * layers
    table = meta_table(sz, recv)
    expand[...] = jnp.zeros(expand.shape, bf16)
    for k in range(3):
        expand[:, k * sz.qw : k * sz.qw + sz.points] = dot(place_terms(sz, k), synthesis[...]).astype(bf16)
    dense = recv[:, : 3 * sz.qw].astype(f32)
    forces[...] = dot(recv[:, 3 * sz.qw :], expand[...])

    stencil = sz.stencil
    dx, dy = table[:stencil], table[stencil : 2 * stencil]
    ax, ay, az = (table[2 * stencil + d : 2 * stencil + d + 1] for d in range(3))
    layer = jnp.floor((az + 0.5) * (1.0 / TILE))
    line = ((ax + dx) * planes + layer) * ny + ay + dy
    line = jnp.where((dx < 0.5 * DEAD) & (ax > 0.5), line, float(gx * planes * ny))
    rows_v[...] = line.astype(jnp.int32)
    copy = pltpu.make_async_copy(rows_v, rows_s, sem)
    copy.start()
    rows_out[...] = rows_v[...]
    for t in range(slots // TILE):
        cols[t] = table[: 2 * stencil, t * TILE : (t + 1) * TILE] * scale

    at = sz.mo + 2 * stencil + 2
    az_col = dense[:, sz.mt + at : sz.mt + at + 1]
    az_col = az_col - TILE * jnp.floor((az_col + 0.5) * (1.0 / TILE))
    points[:, : 2 * sz.qw] = dense[:, : 2 * sz.qw] * scale
    points[:, 2 * sz.qw :] = (dense[:, 2 * sz.qw : 3 * sz.qw] + az_col) * scale

    grid[...] = jnp.zeros(grid.shape, f32)
    y_at = pl.multiple_of(where[1] * nyb, 8)
    for x in range(gx):
        for r in range(planes):
            grid[pl.ds((x * planes + r) * ny + y_at, nyb), :] = vold[pl.ds(x * nyb * planes + r, nyb, stride=planes), :]
    copy.wait()

    def step(g, carry):
        first = pl.multiple_of(g * GROUP, GROUP)
        pts = points[pl.ds(first, GROUP), :]
        frc = forces[pl.ds(first, GROUP), :]
        col = column_group(sz, cols, g)
        for u in range(GROUP):
            cx, cy = col[:stencil, u : u + 1], col[stencil:, u : u + 1]
            total_terms = jnp.zeros((3 * stencil, TILE), f32)
            for t in range(0, sz.qw, TILE):
                w = line_weights(pts[u : u + 1, t : t + TILE], pts[u : u + 1, sz.qw + t : sz.qw + t + TILE], cx, cy)
                weighted = jnp.concatenate(
                    [(frc[u : u + 1, k * sz.qw + t : k * sz.qw + t + TILE] * w).astype(bf16) for k in range(3)], axis=0
                )
                wz = height_weights(pts[u : u + 1, 2 * sz.qw + t : 2 * sz.qw + t + TILE])
                total_terms = total_terms + dot(weighted, wz, 1, 1)
            terms[u] = total_terms
        for u in range(GROUP):
            lines = [rows_s[j, first + u] for j in range(stencil)]
            spots = [pl.ds(line, 3, stride=layers * ny) for line in lines]
            sums = [grid[spots[j], :] + terms[u, pl.ds(j, 3, stride=stencil), :] for j in range(stencil)]
            for j in range(stencil):
                grid[spots[j], :] = sums[j]
        return carry

    lax.fori_loop(0, slots // GROUP, step, 0)

    half = ny // 2
    mine = where[1] % 2
    for p in range(gx * planes):
        keep[p * half : (p + 1) * half] = grid[pl.ds(pl.multiple_of(p * ny + mine * half, 8), half), :].astype(bf16)
        send[p * half : (p + 1) * half] = grid[pl.ds(pl.multiple_of(p * ny + (1 - mine) * half, 8), half), :].astype(bf16)


def sample_kernel(
    sz, gx, ny, nyb, layers, slabs, where, rows_s, own, other, points, cols, analysis,
    vnew, back,
    drive, state, last, expand, gathered, piece, sampled,
):
    planes = 3 * layers
    half = ny // 2
    pad = 8
    wide = gx + 2 * SWEEPS
    edge = jnp.zeros((pad, TILE), f32)
    mine = where[1] % 2

    def load(p, carry):
        for ref, part in ((own, mine), (other, 1 - mine)):
            rows = ref[pl.ds(pl.multiple_of(p * half, 16), half), :].astype(f32)
            drive[p, pl.ds(pl.multiple_of(pad + part * half, 8), half), :] = rows
        for ref in (drive, state):
            ref[p, 0:pad] = edge
            ref[p, pad + ny :] = edge
        return carry

    lax.fori_loop(0, wide * planes, load, 0)

    last_lane = iota((ny, TILE), 1) == TILE - 1
    first_lane = iota((ny, TILE), 1) == 0
    zero = jnp.zeros((ny, TILE), f32)
    inner = pl.ds(pad, ny)

    def sweep(source, p, store):
        for k in range(3):
            centre = [source[(p * 3 + k) * layers + l, inner] for l in range(layers)]
            ahead = [pltpu.roll(c, TILE - 1, 1) for c in centre]
            behind = [pltpu.roll(c, 1, 1) for c in centre]
            for l in range(layers):
                at = (p * 3 + k) * layers + l
                upper = jnp.where(last_lane, ahead[l + 1] if l + 1 < layers else zero, ahead[l])
                lower = jnp.where(first_lane, behind[l - 1] if l else zero, behind[l])
                around = source[at - planes, inner] + source[at + planes, inner]
                around = around + source[at, pl.ds(pad - 1, ny)] + source[at, pl.ds(pad + 1, ny)]
                around = around + upper + lower
                store(at, (drive[at, inner] + coupling * around) * (1.0 / (1.0 + 6.0 * coupling)))

    def first_sweep(p, carry):
        inside = ((p >= SWEEPS) | (where[0] > 0)) & ((p < gx + SWEEPS) | (where[0] < slabs - 1))
        factor = inside.astype(f32)

        def store(at, value):
            state[at, inner] = value * factor

        sweep(drive, p, store)
        return carry

    lax.fori_loop(1, wide - 1, first_sweep, 0)

    def second_sweep(p, carry):
        def store(at, value):
            last[pl.ds(pl.multiple_of((at - SWEEPS * planes) * ny, 8), ny), :] = value

        sweep(state, p, store)
        return carry

    lax.fori_loop(SWEEPS, gx + SWEEPS, second_sweep, 0)
    last[gx * planes * ny :] = jnp.zeros((last.shape[0] - gx * planes * ny, TILE), f32)

    y_at = pl.multiple_of(where[1] * nyb, 8)
    for x in range(gx):
        for r in range(planes):
            vnew[pl.ds(x * nyb * planes + r, nyb, stride=planes), :] = last[pl.ds((x * planes + r) * ny + y_at, nyb), :]

    stencil = sz.stencil
    slots = points.shape[0]

    def step(g, carry):
        first = pl.multiple_of(g * GROUP, GROUP)
        for u in range(GROUP):
            for j in range(stencil):
                spot = pl.ds(rows_s[j, first + u], 3, stride=layers * ny)
                gathered[u, pl.ds(j, 3, stride=stencil), :] = last[spot, :]
        pts = points[pl.ds(first, GROUP), :]
        col = column_group(sz, cols, g)
        for u in range(GROUP):
            cx, cy = col[:stencil, u : u + 1], col[stencil:, u : u + 1]
            tiles = gathered[u].astype(bf16)
            for t in range(0, sz.qw, TILE):
                w = line_weights(pts[u : u + 1, t : t + TILE], pts[u : u + 1, sz.qw + t : sz.qw + t + TILE], cx, cy)
                wz = height_weights(pts[u : u + 1, 2 * sz.qw + t : 2 * sz.qw + t + TILE])
                projected = dot(tiles, wz)
                for k in range(3):
                    part = jnp.sum(projected[k * stencil : (k + 1) * stencil] * w, axis=0, keepdims=True)
                    piece[u : u + 1, k * sz.qw + t : k * sz.qw + t + TILE] = part
        sampled[pl.ds(first, GROUP), :] = piece[...]
        return carry

    lax.fori_loop(0, slots // GROUP, step, 0)

    expand[...] = jnp.zeros(expand.shape, bf16)
    for k in range(3):
        expand[:, k * sz.qw : k * sz.qw + sz.points] = dot(place_terms(sz, k), analysis[...]).astype(bf16)
    back[...] = dot(sampled[...].astype(bf16), expand[...], 1, 1).astype(bf16)


def unpack_kernel(sz, slot, back, out):
    cells, slots = slot.shape[1], back.shape[0]
    place = one_hot(slot[...] == iota((slots, cells), 0))
    coef = dot(place, back[...], 0, 0).astype(bf16)
    for k in range(3):
        shape = (sz.terms, sz.cw)
        pick = one_hot(iota(shape, 1) == iota(shape, 0) + k * sz.terms)
        out[k] = dot(pick, coef, 1, 1).astype(bf16)


def local(
    velocity_old, traction, offsets, owner_slab, anchor, blocks, block_count, synthesis, analysis
):
    cells, _, terms = traction.shape
    gx, nyb, layers = velocity_old.shape[:3]
    slabs, batches = lax.axis_size("slab"), lax.axis_size("batch")
    ny = nyb * batches
    planes = 3 * layers
    cap = 2 * cells // slabs
    slots = slabs * cap
    stencil = blocks.shape[1]
    sz = Sizes(terms, offsets.shape[2], stencil)
    where = jnp.stack([lax.axis_index("slab"), lax.axis_index("batch")]).astype(jnp.int32)

    def shape(dims, dtype):
        return jax.ShapeDtypeStruct(dims, dtype)

    send, slot = pl.pallas_call(
        lambda *refs: pack_kernel(sz, slabs, cap, ny, layers, *refs),
        out_shape=(shape((slots, sz.width), bf16), shape((1, cells), jnp.int32)),
        in_specs=vmem(6),
        out_specs=vmem(2),
        scratch_shapes=[pltpu.VMEM((cells, sz.width), bf16)],
        compiler_params=params,
        name="pack",
    )(
        owner_slab.T,
        anchor.T,
        blocks.T,
        block_count.reshape(1, cells),
        traction.transpose(1, 2, 0),
        offsets.transpose(1, 0, 2),
    )
    recv = lax.all_to_all(send, "slab", split_axis=0, concat_axis=0, tiled=True)

    half = ny // 2
    dump = 3 * layers * ny
    old_rows = velocity_old.transpose(0, 1, 3, 2, 4).reshape(-1, TILE)
    keep, send_half, points, cols, rows = pl.pallas_call(
        lambda *refs: spread_kernel(sz, gx, ny, nyb, layers, *refs),
        out_shape=(
            shape((gx * planes * half, TILE), bf16),
            shape((gx * planes * half, TILE), bf16),
            shape((slots, 3 * sz.qw), f32),
            shape((slots // TILE, 2 * stencil, TILE), f32),
            shape((stencil, slots), jnp.int32),
        ),
        in_specs=smem(1) + vmem(3),
        out_specs=vmem(5),
        scratch_shapes=[
            pltpu.VMEM((gx * planes * ny + dump, TILE), f32),
            pltpu.VMEM((slots, 3 * sz.qw), f32),
            pltpu.VMEM((sz.cw, 3 * sz.qw), bf16),
            pltpu.VMEM((GROUP, 3 * stencil, TILE), f32),
            pltpu.VMEM((stencil, slots), jnp.int32),
            pltpu.SMEM((stencil, slots), jnp.int32),
            pltpu.SemaphoreType.DMA,
        ],
        compiler_params=params,
        name="spread",
    )(where, recv, synthesis, old_rows)

    def pairs(bit):
        return [(i, i ^ bit) for i in range(batches)]

    def add(a, b):
        return (a.astype(f32) + b.astype(f32)).astype(bf16)

    mine = add(keep, lax.ppermute(send_half, "batch", pairs(1)))
    bit = 2
    while bit < batches:
        mine = add(mine, lax.ppermute(mine, "batch", pairs(bit)))
        bit *= 2
    halo = SWEEPS * planes * half
    up = [(i, i + 1) for i in range(slabs - 1)]
    down = [(i + 1, i) for i in range(slabs - 1)]
    low = lax.ppermute(mine[-halo:], "slab", up)
    high = lax.ppermute(mine[:halo], "slab", down)
    mine = jnp.concatenate([low, mine, high], axis=0)
    other = lax.ppermute(mine, "batch", pairs(1))

    wide = gx + 2 * SWEEPS
    vnew, back = pl.pallas_call(
        lambda *refs: sample_kernel(sz, gx, ny, nyb, layers, slabs, *refs),
        out_shape=(
            shape((gx * nyb * planes, TILE), f32),
            shape((slots, sz.cw), bf16),
        ),
        in_specs=smem(2) + vmem(5),
        out_specs=vmem(2),
        scratch_shapes=[
            pltpu.VMEM((wide * planes, ny + 16, TILE), f32),
            pltpu.VMEM((wide * planes, ny + 16, TILE), f32),
            pltpu.VMEM((gx * planes * ny + dump, TILE), f32),
            pltpu.VMEM((sz.cw, 3 * sz.qw), bf16),
            pltpu.VMEM((GROUP, 3 * stencil, TILE), f32),
            pltpu.VMEM((GROUP, 3 * sz.qw), f32),
            pltpu.VMEM((slots, 3 * sz.qw), f32),
        ],
        compiler_params=params,
        name="sample",
    )(where, rows, mine, other, points, cols, analysis)
    velocity_new = vnew.reshape(gx, nyb, 3, layers, TILE).transpose(0, 1, 3, 2, 4)

    returned = lax.all_to_all(back, "slab", split_axis=0, concat_axis=0, tiled=True)
    coef = pl.pallas_call(
        lambda *refs: unpack_kernel(sz, *refs),
        out_shape=shape((3, terms, cells), bf16),
        in_specs=vmem(2),
        out_specs=vmem(1)[0],
        compiler_params=params,
        name="unpack",
    )(slot, returned)
    return velocity_new, coef.transpose(2, 0, 1)


def solution(mesh):
    in_specs = (
        P("slab", "batch", None, None, None),
        P(("slab", "batch"), None, None),
        P(("slab", "batch"), None, None),
        P(("slab", "batch"), None),
        P(("slab", "batch"), None),
        P(("slab", "batch"), None),
        P(("slab", "batch")),
        P(),
        P(),
    )
    out_specs = (P("slab", "batch", None, None, None), P(("slab", "batch"), None, None))
    return jax.shard_map(local, mesh=mesh, in_specs=in_specs, out_specs=out_specs, check_vma=False)
```

```python
import math

import jax
import jax.numpy as jnp
from jax import lax
from jax.experimental import pallas as pl
from jax.experimental.pallas import tpu as pltpu
from jax.sharding import PartitionSpec as P

SWEEPS = 2
TILE = 128
GROUP = 8
MXU_LANES = 256
UNROLL = 6
DEAD = 64.0
MIDDLE = 64.0

kernel_width = 0.8
kernel_norm = 1.0 / (0.8 * math.sqrt(2.0 * math.pi))
coupling = 2.0
square = 0.5 / (math.log(2.0) * kernel_width * kernel_width)
norm_bits = math.log2(kernel_norm)

f32 = jnp.float32
bf16 = jnp.bfloat16


def round_up(value, step):
    return -(-value // step) * step


def iota(shape, dim):
    return lax.broadcasted_iota(jnp.int32, shape, dim)


def one_hot(mask):
    return jnp.where(mask, 1.0, 0.0).astype(bf16)


def dot(a, b, ca=1, cb=0):
    return lax.dot_general(a, b, (((ca,), (cb,)), ((), ())), preferred_element_type=f32)


def vmem(count=1):
    return [pl.BlockSpec(memory_space=pltpu.VMEM)] * count


def smem(count=1):
    return [pl.BlockSpec(memory_space=pltpu.SMEM)] * count


params = pltpu.CompilerParams(vmem_limit_bytes=12 * 1024 * 1024)


class Sizes:
    def __init__(self, terms, points, stencil):
        self.terms, self.points, self.stencil = terms, points, stencil
        self.qw = round_up(points, TILE)
        self.cw = round_up(3 * terms, TILE)
        self.width = 3 * self.qw + self.cw
        self.mt = points // TILE * TILE
        self.mo = points - self.mt
        self.meta = 2 * stencil + 3
        self.rows = round_up(self.meta, 8)


def place_terms(sz, k):
    shape = (sz.cw, sz.terms)
    return one_hot(iota(shape, 0) == iota(shape, 1) + k * sz.terms)


def pieces(value, count):
    out = []
    for _ in range(count):
        part = value.astype(bf16).astype(f32)
        out.append(part)
        value = value - part
    return out


def pack_kernel(sz, slabs, cap, chunks, pairwise, ny, layers, *refs):
    where, owner, anchor, blocks, count, trac, offs = refs[:7]
    send, slot_out, rec = refs[7 : 7 + chunks], refs[7 + chunks], refs[8 + chunks]
    cells = owner.shape[1]
    slots = slabs * cap
    own = owner[...]
    member = one_hot(own == iota((slabs, cells), 0))
    before = one_hot(iota((cells, cells), 0) < iota((cells, cells), 1))
    rank = jnp.sum(member.astype(f32) * dot(member, before), axis=0, keepdims=True)
    if pairwise:
        slot = (own ^ where[0]) * cap + rank.astype(jnp.int32)
    else:
        part = cap // chunks
        chunk = jnp.floor((rank + 0.5) * (1.0 / part))
        slot = (chunk * (slabs * part - part) + rank).astype(jnp.int32) + own * part
    slot_out[...] = slot
    place = one_hot(slot == iota((slots, cells), 0))

    tile = blocks[...].astype(f32)
    anchors = anchor[...].astype(f32)
    tile_x = jnp.floor((tile + 0.5) * (1.0 / (ny * layers)))
    tile_y = jnp.floor((tile + 0.5) * (1.0 / layers)) - tile_x * ny
    live = iota(tile.shape, 0) < count[...]
    dx = jnp.where(live, tile_x - anchors[0:1], DEAD)
    dy = jnp.where(live, tile_y - anchors[1:2], DEAD)

    rec[...] = jnp.zeros(rec.shape, bf16)
    for k in range(3):
        rec[:, k * sz.qw : k * sz.qw + sz.points] = offs[k]
    base = sz.mo
    meta = jnp.zeros((cells, TILE), f32)
    for row in (dx, dy, anchors):
        shape = (row.shape[0], TILE)
        where = one_hot(iota(shape, 1) == iota(shape, 0) + base)
        meta = meta + dot(row.astype(bf16), where, 0, 0)
        base += row.shape[0]
    rec[:, sz.mt : sz.mt + TILE] = rec[:, sz.mt : sz.mt + TILE] + meta.astype(bf16)
    coef = jnp.zeros((cells, sz.cw), f32)
    for k in range(3):
        coef = coef + dot(trac[k], place_terms(sz, k), 0, 1)
    rec[:, 3 * sz.qw :] = coef.astype(bf16)
    size = slots // chunks
    for c in range(chunks):
        send[c][...] = dot(place[c * size : (c + 1) * size], rec[...]).astype(bf16)


def load_records(sz, recv, points, lines):
    stencil = sz.stencil
    base = 0
    shape = (TILE, TILE)
    for part in recv:
        slots = part.shape[0]
        points[base : base + slots] = part[:, : 3 * sz.qw].astype(f32)
        meta = part[:, sz.mt : sz.mt + TILE]
        az = dot(meta, one_hot(iota(shape, 0) == sz.mo + 2 * stencil + 2))
        height = az - TILE * jnp.floor((az + 0.5) * (1.0 / TILE)) - MIDDLE
        for t in range(2 * sz.qw, 3 * sz.qw, TILE):
            points[base : base + slots, t : t + TILE] = points[base : base + slots, t : t + TILE] + height
        groups = slots // GROUP
        merge = one_hot(iota((groups, slots), 0) == iota((groups, slots), 1) // GROUP)
        mine = iota((slots, TILE), 0) % GROUP == iota((slots, TILE), 1) // stencil
        for d in range(2):
            spread = one_hot(iota(shape, 0) == iota(shape, 1) % stencil + sz.mo + d * stencil)
            lines[d, base // GROUP : base // GROUP + groups] = dot(
                merge, jnp.where(mine, dot(meta, spread), 0.0).astype(bf16)
            )
        base += slots


def height_table(shape, dim):
    cell, height = iota(shape, dim) // TILE, iota(shape, dim) % TILE
    kind, mine = iota(shape, 1 - dim) // GROUP, iota(shape, 1 - dim) % GROUP == cell
    m = height.astype(f32) - MIDDLE
    minus = pieces(-square * m * m, 3)
    value = jnp.where(kind < 3, m, jnp.where(kind < 6, 1.0, 0.0))
    for i in range(3):
        value = jnp.where(kind == 6 + i, minus[i], value)
    return jnp.where(mine, value, 0.0).astype(bf16)


def stack_rows(rows, like):
    rows = rows + [jnp.zeros_like(like)] * (TILE // GROUP - len(rows))
    return jnp.concatenate(rows, axis=0).astype(bf16)


def line_weights(sz, g, points, lines, w_ref):
    first = pl.multiple_of(g * GROUP, GROUP)
    pts = points[pl.ds(first, GROUP), : 2 * sz.qw]
    ox, oy = pts[:, : sz.qw], pts[:, sz.qw :]
    steps = [lines[d, pl.ds(g, 1), :] for d in range(2)]
    mine = iota((GROUP, TILE), 0) == iota((GROUP, TILE), 1) // sz.stencil
    dx, dy, norm = (jnp.where(mine, value, 0.0) for value in (*steps, steps[0] * steps[0] + steps[1] * steps[1]))
    unit = jnp.where(mine, 1.0, 0.0)
    left = stack_rows([dx, dx, dy, dy, unit, unit, norm, norm], dx)
    rows = pieces(2.0 * square * ox, 2) + pieces(2.0 * square * oy, 2)
    rows = rows + pieces(2.0 * norm_bits - square * (ox * ox + oy * oy), 2)
    rows = rows + pieces(jnp.full_like(ox, -square), 2)
    w_ref[...] = jnp.exp2(dot(left, stack_rows(rows, ox), 0, 0))


def height_factors(oz):
    rows = pieces(2.0 * square * oz, 3) + pieces(norm_bits - square * oz * oz, 3) + [jnp.ones_like(oz)] * 3
    return stack_rows(rows, oz)


def basis_kernel(sz, synthesis, analysis, spread_out, sample_out, spread_table, sample_table):
    for basis, out in ((synthesis, spread_out), (analysis, sample_out)):
        out[...] = jnp.zeros(out.shape, bf16)
        for k in range(3):
            out[:, k * sz.qw : k * sz.qw + sz.points] = dot(place_terms(sz, k), basis[...]).astype(bf16)
    spread_table[...] = height_table(spread_table.shape, 1)
    sample_table[...] = height_table(sample_table.shape, 0)


def in_turn(*works):
    works = list(works)
    while works:
        works = [work for work in works if next(work, works) is not works]


def run_groups(count, prepare, use, slots):
    in_turn(prepare(0, *slots[0]))
    turns = next(t for t in (UNROLL, 4, 2, 1) if count % t == 0)

    def step(h, carry):
        for i in range(turns):
            g = turns * h + i
            if turns % 2:
                in_turn(use(g, *slots[0]))
                in_turn(prepare(g + 1, *slots[0]))
            else:
                in_turn(prepare(g + 1, *slots[(i + 1) % 2]), use(g, *slots[i % 2]))
        return carry

    lax.fori_loop(0, count // turns, step, 0)


def stencil_rows(sz, gx, ny, layers, meta):
    stencil, planes = sz.stencil, 3 * layers
    shape = (TILE, TILE)
    source, lane = iota(shape, 0) - sz.mo, iota(shape, 1)
    dx, dy = (dot(meta, one_hot((source == lane + d * stencil) & (lane < stencil))) for d in range(2))
    ax, ay, az = (dot(meta, one_hot(source == 2 * stencil + d)) for d in range(3))
    layer = jnp.floor((az + 0.5) * (1.0 / TILE))
    line = ((ax + dx) * ny + ay + dy) * planes + layer
    line = jnp.where((dx < 0.5 * DEAD) & (ax > 0.5), line, float(gx * planes * ny))
    return line


def spread_kernel(sz, gx, ny, nyb, layers, parts, begin, end, *refs):
    where, recv, (expand, table, start), refs = refs[0], refs[1 : 1 + parts], refs[1 + parts : 4 + parts], refs[4 + parts :]
    grid, rows_out = refs[0], refs[1 : 1 + parts]
    if end:
        keep, send = refs[1 + parts : 3 + parts]
    points, lines, forces, w0, wz0, w1, wz1, terms, rows_s, sem = refs[(3 if end else 1) + parts :]
    slots = points.shape[0]
    planes = 3 * layers
    stencil = sz.stencil
    count = slots // GROUP

    copies = []
    for i, part in enumerate(recv):
        size = part.shape[0]
        meta = part[:, sz.mt : sz.mt + TILE]
        rows_out[i][...] = stencil_rows(sz, gx, ny, layers, meta).astype(jnp.int32)
        copies.append(pltpu.make_async_copy(rows_out[i], rows_s.at[pl.ds(i * size, size)], sem.at[i]))
        copies[-1].start()
    load_records(sz, recv, points, lines)
    base = 0
    for part in recv:
        size = part.shape[0]
        forces[base : base + size] = dot(part[:, 3 * sz.qw :], expand[...])
        base += size
    if begin:
        grid[...] = jnp.zeros(grid.shape, f32)
        size = nyb * planes
        for x in range(gx):
            grid[pl.ds(pl.multiple_of(x * ny * planes + where[1] * size, 8), size), :] = start[x * size : (x + 1) * size]
    for copy in copies:
        copy.wait()

    def prepare(g, w_ref, wz_ref):
        g = jnp.minimum(g, count - 1)
        line_weights(sz, g, points, lines, w_ref)
        oz = points[pl.ds(pl.multiple_of(g * GROUP, GROUP), GROUP), 2 * sz.qw :]
        left = jnp.transpose(height_factors(oz))
        yield
        for u in range(0, GROUP * TILE, 2 * TILE):
            for t in range(0, sz.qw, TILE):
                exponents = dot(left[t : t + TILE], table[:, u : u + 2 * TILE])
                wz_ref[t : t + TILE, u : u + 2 * TILE] = jnp.exp2(exponents).astype(bf16)
                yield

    def use(g, w_ref, wz_ref):
        first = pl.multiple_of(g * GROUP, GROUP)
        frc = forces[pl.ds(first, GROUP), :]
        for u in range(GROUP):
            w = w_ref[u * stencil : (u + 1) * stencil]
            weighted = [(frc[u : u + 1, k * sz.qw : (k + 1) * sz.qw] * w).astype(bf16) for k in range(3)]
            sums = dot(jnp.concatenate(weighted, axis=0), wz_ref[:, u * TILE : (u + 1) * TILE])
            for k in range(3):
                for j in range(0, stencil, 8):
                    terms[u, pl.ds(4 * j + k, 8, stride=4), :] = sums[k * stencil + j : k * stencil + j + 8]
            yield
            spots = [pl.ds(rows_s[first + u, j], 3, stride=layers) for j in range(stencil)]
            sums = [grid[spots[j], :] + terms[u, 4 * j : 4 * j + 3] for j in range(stencil)]
            for j in range(stencil):
                grid[spots[j], :] = sums[j]

    run_groups(count, prepare, use, ((w0, wz0), (w1, wz1)))

    if end:
        half = ny // 2 * planes
        mine = where[1] % 2
        for x in range(gx):
            for ref, part in ((keep, mine), (send, 1 - mine)):
                rows = grid[pl.ds(pl.multiple_of((2 * x + part) * half, 8), half), :]
                ref[x * half : (x + 1) * half] = rows.astype(bf16)


def relax(gx, ny, layers, slabs, where, own, other, drive, state, last):
    planes = 3 * layers
    rows = ny * planes
    half = rows // 2
    pad = (drive.shape[1] - rows) // 2
    wide = gx + 2 * SWEEPS
    edge = jnp.zeros((pad, TILE), f32)
    mine = where[1] % 2

    def load(p, carry):
        for ref, part in ((own, mine), (other, 1 - mine)):
            values = ref[pl.ds(pl.multiple_of(p * half, 16), half), :].astype(f32)
            drive[p, pl.ds(pl.multiple_of(pad + part * half, 8), half), :] = values
        for ref in (drive, state):
            ref[p, 0:pad] = edge
            ref[p, pad + rows :] = edge
        return carry

    lax.fori_loop(0, wide, load, 0)

    size = 8 * planes
    lane = iota((size, TILE), 1)
    layer = iota((size, TILE), 0) % layers
    last_lane, first_lane = lane == TILE - 1, lane == 0
    above = jnp.where(layer < layers - 1, 1.0, 0.0)
    below = jnp.where(layer > 0, 1.0, 0.0)

    def sweep(source, p, store):
        for at in range(0, rows, size):
            def near(step):
                return source[p, pl.ds(pad + at + step, size), :]

            upper = pltpu.roll(jnp.where(first_lane, near(1) * above, near(0)), TILE - 1, 1)
            lower = pltpu.roll(jnp.where(last_lane, near(-1) * below, near(0)), 1, 1)
            around = source[p - 1, pl.ds(pad + at, size), :] + source[p + 1, pl.ds(pad + at, size), :]
            around = around + near(planes) + near(-planes) + upper + lower
            centre = drive[p, pl.ds(pad + at, size), :]
            store(p, at, (centre + coupling * around) * (1.0 / (1.0 + 6.0 * coupling)))

    def first_sweep(p, carry):
        inside = ((p >= SWEEPS) | (where[0] > 0)) & ((p < gx + SWEEPS) | (where[0] < slabs - 1))
        factor = inside.astype(f32)

        def store(p, at, value):
            state[p, pl.ds(pad + at, size), :] = value * factor

        sweep(drive, p, store)
        return carry

    lax.fori_loop(1, wide - 1, first_sweep, 0)

    def second_sweep(p, carry):
        def store(p, at, value):
            last[pl.ds(pl.multiple_of((p - SWEEPS) * rows + at, 8), size), :] = value

        sweep(state, p, store)
        return carry

    lax.fori_loop(SWEEPS, gx + SWEEPS, second_sweep, 0)
    last[gx * rows :] = jnp.zeros((last.shape[0] - gx * rows, TILE), f32)


def sample_kernel(sz, gx, ny, nyb, layers, slabs, parts, begin, *refs):
    lines_in, recv, (expand, table), refs = refs[:parts], refs[parts : 2 * parts], refs[2 * parts : 2 + 2 * parts], refs[2 + 2 * parts :]
    if begin:
        where, own, other, last, vnew = refs[:5]
        back, (drive, state), refs = refs[5 : 5 + parts], refs[5 + parts : 7 + parts], refs[7 + parts :]
    else:
        last, back, refs = refs[0], refs[1 : 1 + parts], refs[1 + parts :]
    points, lines, w0, wz0, w1, wz1, gathered, products, sampled, rows_s, sem = refs
    copies = []
    for i, part in enumerate(lines_in):
        size = part.shape[0]
        copies.append(pltpu.make_async_copy(part, rows_s.at[pl.ds(i * size, size)], sem.at[i]))
        copies[-1].start()
    stencil = sz.stencil
    slots = points.shape[0]
    count = slots // GROUP
    planes = 3 * layers
    load_records(sz, recv, points, lines)
    if begin:
        relax(gx, ny, layers, slabs, where, own, other, drive, state, last)
        size = nyb * planes
        for x in range(gx):
            at = pl.multiple_of(x * ny * planes + where[1] * size, 8)
            vnew[x * size : (x + 1) * size] = last[pl.ds(at, size), :]
    shape = (3 * GROUP, 3 * GROUP * stencil)
    cell, part = iota(shape, 1) // (3 * stencil), iota(shape, 1) // stencil % 3
    adds = one_hot(iota(shape, 0) == part * GROUP + cell)

    for copy in copies:
        copy.wait()
    cut = sz.qw // MXU_LANES * MXU_LANES
    heights = (iota((TILE, TILE), 0).astype(f32) - MIDDLE) * math.sqrt(square)

    def prepare(g, w_ref, wz_ref):
        g = jnp.minimum(g, count - 1)
        line_weights(sz, g, points, lines, w_ref)
        oz = points[pl.ds(pl.multiple_of(g * GROUP, GROUP), GROUP), 2 * sz.qw :]
        right = height_factors(oz[:, :cut]) if cut else None
        rest = oz[:, cut:] * math.sqrt(square)
        yield
        for u in range(GROUP):
            if cut:
                exponents = dot(table[u * TILE : (u + 1) * TILE], right)
                wz_ref[u * TILE : (u + 1) * TILE, :cut] = jnp.exp2(exponents).astype(bf16)
            for t in range(cut, sz.qw, TILE):
                away = rest[u : u + 1, t - cut : t - cut + TILE] - heights
                value = jnp.exp2(norm_bits - away * away).astype(bf16)
                wz_ref[u * TILE : (u + 1) * TILE, t : t + TILE] = value
            yield

    def use(g, w_ref, wz_ref):
        first = pl.multiple_of(g * GROUP, GROUP)
        for u in range(GROUP):
            for j in range(stencil):
                spot = pl.ds(rows_s[first + u, j], 3, stride=layers)
                gathered[u, 4 * j : 4 * j + 3] = last[spot, :]
        for u in range(GROUP):
            tiles = [
                gathered[u, pl.ds(4 * j + k, 8, stride=4), :] for k in range(3) for j in range(0, stencil, 8)
            ]
            projected = dot(jnp.concatenate(tiles, axis=0).astype(bf16), wz_ref[u * TILE : (u + 1) * TILE])
            w = w_ref[u * stencil : (u + 1) * stencil]
            for k in range(3):
                at = (u * 3 + k) * stencil
                products[at : at + stencil] = (projected[k * stencil : (k + 1) * stencil] * w).astype(bf16)
            yield
        values = dot(adds, products[...])
        for k in range(3):
            sampled[pl.ds(first, GROUP), k * sz.qw : (k + 1) * sz.qw] = values[k * GROUP : (k + 1) * GROUP]

    run_groups(count, prepare, use, ((w0, wz0), (w1, wz1)))
    base = 0
    for ref in back:
        size = ref.shape[0]
        ref[...] = dot(sampled[base : base + size].astype(bf16), expand[...], 1, 1).astype(bf16)
        base += size


def unpack_kernel(sz, *refs):
    slot, out = refs[0], refs[-1]
    parts = refs[1:-1]
    cells, size = slot.shape[1], parts[0].shape[0]
    coef = jnp.zeros((cells, sz.cw), f32)
    for c, back in enumerate(parts):
        place = one_hot(slot[...] == iota((size, cells), 0) + c * size)
        coef = coef + dot(place, back[...], 0, 0)
    coef = coef.astype(bf16)
    for k in range(3):
        shape = (sz.terms, sz.cw)
        pick = one_hot(iota(shape, 1) == iota(shape, 0) + k * sz.terms)
        out[k] = dot(pick, coef, 1, 1).astype(bf16)


def local(
    velocity_old, traction, offsets, owner_slab, anchor, blocks, block_count, synthesis, analysis
):
    cells, _, terms = traction.shape
    gx, nyb, layers = velocity_old.shape[:3]
    slabs, batches = lax.axis_size("slab"), lax.axis_size("batch")
    ny = nyb * batches
    planes = 3 * layers
    cap = 2 * cells // slabs
    stencil = blocks.shape[1]
    sz = Sizes(terms, offsets.shape[2], stencil)
    where = jnp.stack([lax.axis_index("slab"), lax.axis_index("batch")]).astype(jnp.int32)
    half = ny // 2
    grid_rows = gx * ny * planes + 8 * planes

    pairwise = cap % 16 == 0 and slabs & (slabs - 1) == 0
    if pairwise:
        chunks, size = slabs, cap
        stages = [list(range(min(4, slabs)))] + ([list(range(4, slabs))] if slabs > 4 else [])
        back_stages = [list(range(4, slabs)), list(range(1, min(4, slabs))), [0]]
        back_stages = [stage for stage in back_stages if stage]
    else:
        chunks = next(c for c in (3, 2, 1) if cap % c == 0 and slabs * (cap // c) % 16 == 0)
        size = slabs * cap // chunks
        stages = back_stages = [[c] for c in range(chunks)]

    def exchange(value, p):
        if not pairwise:
            return lax.all_to_all(value, "slab", split_axis=0, concat_axis=0, tiled=True)
        return lax.ppermute(value, "slab", [(i, i ^ p) for i in range(slabs)]) if p else value

    def shape(dims, dtype):
        return jax.ShapeDtypeStruct(dims, dtype)

    def whole(dims):
        return pl.BlockSpec(dims, lambda i: (0,) * len(dims))

    packed = [
        owner_slab.T,
        anchor.T,
        blocks.T,
        block_count.reshape(1, cells),
        traction.transpose(1, 2, 0),
        offsets.transpose(1, 0, 2),
    ]
    send = pl.pallas_call(
        lambda *refs: pack_kernel(sz, slabs, cap, chunks, pairwise, ny, layers, *refs),
        grid=(1,),
        out_shape=[shape((size, sz.width), bf16)] * chunks + [shape((1, cells), jnp.int32)],
        in_specs=smem(1) + [whole(value.shape) for value in packed],
        out_specs=[whole((size, sz.width))] * chunks + [whole((1, cells))],
        scratch_shapes=[pltpu.VMEM((cells, sz.width), bf16)],
        compiler_params=pltpu.CompilerParams(vmem_limit_bytes=60 * 1024 * 1024),
        name="pack",
    )(where, *packed)
    slot = send[chunks]
    recv = [exchange(send[p], p) for p in range(chunks)]

    expand_shape = shape((sz.cw, 3 * sz.qw), bf16)
    spread_basis, sample_basis, spread_table, sample_table = pl.pallas_call(
        lambda *refs: basis_kernel(sz, *refs),
        out_shape=[expand_shape, expand_shape, shape((TILE, GROUP * TILE), bf16), shape((GROUP * TILE, TILE), bf16)],
        in_specs=vmem(2),
        out_specs=vmem(4),
        compiler_params=params,
        name="basis",
    )(synthesis, analysis)

    grid_shape = shape((grid_rows, TILE), f32)
    half_shape = shape((gx * planes * half, TILE), bf16)
    weights_xy = pltpu.VMEM((GROUP * stencil, sz.qw), f32)
    terms_shape = pltpu.VMEM((GROUP, 4 * stencil, TILE), f32)
    grid = velocity_old.transpose(0, 1, 3, 2, 4).reshape(-1, TILE)
    rows = {}
    for stage in stages:
        parts = len(stage)
        slots = parts * size
        begin, end = stage is stages[0], stage is stages[-1]
        points = [pltpu.VMEM((slots, 3 * sz.qw), f32), pltpu.VMEM((2, slots // GROUP, TILE), f32)]
        out = pl.pallas_call(
            lambda *refs: spread_kernel(sz, gx, ny, nyb, layers, parts, begin, end, *refs),
            out_shape=[
                grid_shape,
            ]
            + [shape((size, TILE), jnp.int32)] * parts
            + [half_shape] * (2 * end),
            in_specs=smem(1) + vmem(parts + 3),
            out_specs=vmem(1 + parts + 2 * end),
            scratch_shapes=points
            + [pltpu.VMEM((slots, 3 * sz.qw), f32)]
            + [weights_xy, pltpu.VMEM((sz.qw, GROUP * TILE), bf16)] * 2
            + [terms_shape, pltpu.SMEM((slots, TILE), jnp.int32), pltpu.SemaphoreType.DMA((parts,))],
            input_output_aliases={} if begin else {3 + parts: 0},
            compiler_params=params,
            cost_estimate=pl.CostEstimate(flops=100_000_000 * slots, bytes_accessed=4_000_000, transcendentals=0),
            name="spread",
        )(where, *(recv[p] for p in stage), spread_basis, spread_table, grid)
        grid = out[0]
        rows.update(zip(stage, out[1 : 1 + parts]))
    keep, send_half = out[-2:]

    def pairs(bit):
        return [(i, i ^ bit) for i in range(batches)]

    def add(a, b):
        return (a.astype(f32) + b.astype(f32)).astype(bf16)

    mine = add(keep, lax.ppermute(send_half, "batch", pairs(1)))
    bit = 2
    while bit < batches:
        mine = add(mine, lax.ppermute(mine, "batch", pairs(bit)))
        bit *= 2
    halo = SWEEPS * planes * half
    up = [(i, i + 1) for i in range(slabs - 1)]
    down = [(i + 1, i) for i in range(slabs - 1)]
    low = lax.ppermute(mine[-halo:], "slab", up)
    high = lax.ppermute(mine[:halo], "slab", down)
    mine = jnp.concatenate([low, mine, high], axis=0)
    other = lax.ppermute(mine, "batch", pairs(1))

    wide = gx + 2 * SWEEPS
    padded = pltpu.VMEM((wide, planes * ny + 16, TILE), f32)
    returned = [None] * chunks
    for stage in back_stages:
        parts = len(stage)
        slots = parts * size
        begin = stage is back_stages[0]
        out = pl.pallas_call(
            lambda *refs: sample_kernel(sz, gx, ny, nyb, layers, slabs, parts, begin, *refs),
            out_shape=([grid_shape, shape((gx * nyb * planes, TILE), f32)] if begin else [])
            + [shape((size, sz.cw), bf16)] * parts,
            in_specs=vmem(2 * parts + 2) + (smem(1) + vmem(2) if begin else vmem(1)),
            out_specs=vmem(2 * begin + parts),
            scratch_shapes=([padded, padded] if begin else [])
            + [pltpu.VMEM((slots, 3 * sz.qw), f32), pltpu.VMEM((2, slots // GROUP, TILE), f32)]
            + [weights_xy, pltpu.VMEM((GROUP * TILE, sz.qw), bf16)] * 2
            + [terms_shape]
            + [pltpu.VMEM((3 * GROUP * stencil, sz.qw), bf16), pltpu.VMEM((slots, 3 * sz.qw), f32)]
            + [pltpu.SMEM((slots, TILE), jnp.int32), pltpu.SemaphoreType.DMA((parts,))],
            compiler_params=params,
            cost_estimate=pl.CostEstimate(flops=50_000_000 * slots, bytes_accessed=4_000_000, transcendentals=0),
            name="sample",
        )(*(rows[p] for p in stage), *(recv[p] for p in stage), sample_basis, sample_table, *((where, mine, other) if begin else (grid,)))
        if begin:
            grid, vnew = out[:2]
        for p, back in zip(stage, out[2 * begin :]):
            returned[p] = exchange(back, p)
    velocity_new = vnew.reshape(gx, nyb, 3, layers, TILE).transpose(0, 1, 3, 2, 4)

    coef = pl.pallas_call(
        lambda *refs: unpack_kernel(sz, *refs),
        out_shape=shape((3, terms, cells), bf16),
        in_specs=vmem(1 + chunks),
        out_specs=vmem(1)[0],
        compiler_params=params,
        name="unpack",
    )(slot, *returned)
    return velocity_new, coef.transpose(2, 0, 1)


def solution(mesh):
    in_specs = (
        P("slab", "batch", None, None, None),
        P(("slab", "batch"), None, None),
        P(("slab", "batch"), None, None),
        P(("slab", "batch"), None),
        P(("slab", "batch"), None),
        P(("slab", "batch"), None),
        P(("slab", "batch")),
        P(),
        P(),
    )
    out_specs = (P("slab", "batch", None, None, None), P(("slab", "batch"), None, None))
    return jax.shard_map(local, mesh=mesh, in_specs=in_specs, out_specs=out_specs, check_vma=False)
```

```python
import math

import jax
import jax.numpy as jnp
from jax import lax
from jax.experimental import pallas as pl
from jax.experimental.pallas import tpu as pltpu
from jax.sharding import PartitionSpec as P

SWEEPS = 2
TILE = 128
GROUP = 8
MXU_LANES = 256
UNROLL = 6
DEAD = 64.0
MIDDLE = 64.0

kernel_width = 0.8
kernel_norm = 1.0 / (0.8 * math.sqrt(2.0 * math.pi))
coupling = 2.0
square = 0.5 / (math.log(2.0) * kernel_width * kernel_width)
norm_bits = math.log2(kernel_norm)

f32 = jnp.float32
bf16 = jnp.bfloat16


def round_up(value, step):
    return -(-value // step) * step


def iota(shape, dim):
    return lax.broadcasted_iota(jnp.int32, shape, dim)


def one_hot(mask):
    return jnp.where(mask, 1.0, 0.0).astype(bf16)


def dot(a, b, ca=1, cb=0):
    return lax.dot_general(a, b, (((ca,), (cb,)), ((), ())), preferred_element_type=f32)


def vmem(count=1):
    return [pl.BlockSpec(memory_space=pltpu.VMEM)] * count


params = pltpu.CompilerParams(vmem_limit_bytes=12 * 1024 * 1024)


class Sizes:
    def __init__(self, terms, points, stencil):
        self.terms, self.points, self.stencil = terms, points, stencil
        self.qw = round_up(points, TILE)
        self.cw = round_up(3 * terms, TILE)
        self.width = 3 * self.qw + self.cw
        self.mt = points // TILE * TILE
        self.mo = points - self.mt
        self.meta = 2 * stencil + 3
        self.rows = round_up(self.meta, 8)


def place_terms(sz, k):
    shape = (sz.cw, sz.terms)
    return one_hot(iota(shape, 0) == iota(shape, 1) + k * sz.terms)


def pieces(value, count):
    out = []
    for _ in range(count):
        part = value.astype(bf16).astype(f32)
        out.append(part)
        value = value - part
    return out


def pack_kernel(sz, slabs, cap, chunks, pairwise, ny, layers, *refs):
    owner, anchor, blocks, count, trac, offs = refs[:6]
    send, slot_out, rec = refs[6 : 6 + chunks], refs[6 + chunks], refs[7 + chunks]
    cells = owner.shape[1]
    slots = slabs * cap
    own = owner[...]
    member = one_hot(own == iota((slabs, cells), 0))
    before = one_hot(iota((cells, cells), 0) < iota((cells, cells), 1))
    rank = jnp.sum(member.astype(f32) * dot(member, before), axis=0, keepdims=True)
    if pairwise:
        slot = (own ^ lax.axis_index("slab")) * cap + rank.astype(jnp.int32)
    else:
        part = cap // chunks
        chunk = jnp.floor((rank + 0.5) * (1.0 / part))
        slot = (chunk * (slabs * part - part) + rank).astype(jnp.int32) + own * part
    slot_out[...] = slot
    place = one_hot(slot == iota((slots, cells), 0))

    tile = blocks[...].astype(f32)
    anchors = anchor[...].astype(f32)
    tile_x = jnp.floor((tile + 0.5) * (1.0 / (ny * layers)))
    tile_y = jnp.floor((tile + 0.5) * (1.0 / layers)) - tile_x * ny
    live = iota(tile.shape, 0) < count[...]
    dx = jnp.where(live, tile_x - anchors[0:1], DEAD)
    dy = jnp.where(live, tile_y - anchors[1:2], DEAD)

    rec[...] = jnp.zeros(rec.shape, bf16)
    for k in range(3):
        rec[:, k * sz.qw : k * sz.qw + sz.points] = offs[k]
    base = sz.mo
    meta = jnp.zeros((cells, TILE), f32)
    for row in (dx, dy, anchors):
        shape = (row.shape[0], TILE)
        where = one_hot(iota(shape, 1) == iota(shape, 0) + base)
        meta = meta + dot(row.astype(bf16), where, 0, 0)
        base += row.shape[0]
    rec[:, sz.mt : sz.mt + TILE] = rec[:, sz.mt : sz.mt + TILE] + meta.astype(bf16)
    coef = jnp.zeros((cells, sz.cw), f32)
    for k in range(3):
        coef = coef + dot(trac[k], place_terms(sz, k), 0, 1)
    rec[:, 3 * sz.qw :] = coef.astype(bf16)
    size = slots // chunks
    for c in range(chunks):
        send[c][...] = dot(place[c * size : (c + 1) * size], rec[...]).astype(bf16)


def load_records(sz, recv, points, lines):
    stencil = sz.stencil
    base = 0
    shape = (TILE, TILE)
    for part in recv:
        slots = part.shape[0]
        points[base : base + slots] = part[:, : 3 * sz.qw].astype(f32)
        meta = part[:, sz.mt : sz.mt + TILE]
        az = dot(meta, one_hot(iota(shape, 0) == sz.mo + 2 * stencil + 2))
        height = az - TILE * jnp.floor((az + 0.5) * (1.0 / TILE)) - MIDDLE
        for t in range(2 * sz.qw, 3 * sz.qw, TILE):
            points[base : base + slots, t : t + TILE] = points[base : base + slots, t : t + TILE] + height
        groups = slots // GROUP
        merge = one_hot(iota((groups, slots), 0) == iota((groups, slots), 1) // GROUP)
        mine = iota((slots, TILE), 0) % GROUP == iota((slots, TILE), 1) // stencil
        for d in range(2):
            spread = one_hot(iota(shape, 0) == iota(shape, 1) % stencil + sz.mo + d * stencil)
            lines[d, base // GROUP : base // GROUP + groups] = dot(
                merge, jnp.where(mine, dot(meta, spread), 0.0).astype(bf16)
            )
        base += slots


def height_table(shape, dim):
    cell, height = iota(shape, dim) // TILE, iota(shape, dim) % TILE
    kind, mine = iota(shape, 1 - dim) // GROUP, iota(shape, 1 - dim) % GROUP == cell
    m = height.astype(f32) - MIDDLE
    minus = pieces(-square * m * m, 3)
    value = jnp.where(kind < 3, m, jnp.where(kind < 6, 1.0, 0.0))
    for i in range(3):
        value = jnp.where(kind == 6 + i, minus[i], value)
    return jnp.where(mine, value, 0.0).astype(bf16)


def stack_rows(rows, like):
    rows = rows + [jnp.zeros_like(like)] * (TILE // GROUP - len(rows))
    return jnp.concatenate(rows, axis=0).astype(bf16)


def line_weights(sz, g, points, lines, w_ref):
    first = pl.multiple_of(g * GROUP, GROUP)
    pts = points[pl.ds(first, GROUP), : 2 * sz.qw]
    ox, oy = pts[:, : sz.qw], pts[:, sz.qw :]
    steps = [lines[d, pl.ds(g, 1), :] for d in range(2)]
    mine = iota((GROUP, TILE), 0) == iota((GROUP, TILE), 1) // sz.stencil
    dx, dy, norm = (jnp.where(mine, value, 0.0) for value in (*steps, steps[0] * steps[0] + steps[1] * steps[1]))
    unit = jnp.where(mine, 1.0, 0.0)
    left = stack_rows([dx, dx, dy, dy, unit, unit, norm, norm], dx)
    rows = pieces(2.0 * square * ox, 2) + pieces(2.0 * square * oy, 2)
    rows = rows + pieces(2.0 * norm_bits - square * (ox * ox + oy * oy), 2)
    rows = rows + pieces(jnp.full_like(ox, -square), 2)
    w_ref[...] = jnp.exp2(dot(left, stack_rows(rows, ox), 0, 0))


def height_factors(oz):
    rows = pieces(2.0 * square * oz, 3) + pieces(norm_bits - square * oz * oz, 3) + [jnp.ones_like(oz)] * 3
    return stack_rows(rows, oz)


def basis_kernel(sz, synthesis, analysis, spread_out, sample_out, spread_table, sample_table):
    for basis, out in ((synthesis, spread_out), (analysis, sample_out)):
        out[...] = jnp.zeros(out.shape, bf16)
        for k in range(3):
            out[:, k * sz.qw : k * sz.qw + sz.points] = dot(place_terms(sz, k), basis[...]).astype(bf16)
    spread_table[...] = height_table(spread_table.shape, 1)
    sample_table[...] = height_table(sample_table.shape, 0)


def in_turn(*works):
    works = list(works)
    while works:
        works = [work for work in works if next(work, works) is not works]


def run_groups(count, prepare, use, slots):
    in_turn(prepare(0, *slots[0]))
    turns = next(t for t in (UNROLL, 4, 2, 1) if count % t == 0)

    def step(h, carry):
        for i in range(turns):
            g = turns * h + i
            if turns % 2:
                in_turn(use(g, *slots[0]))
                in_turn(prepare(g + 1, *slots[0]))
            else:
                in_turn(prepare(g + 1, *slots[(i + 1) % 2]), use(g, *slots[i % 2]))
        return carry

    lax.fori_loop(0, count // turns, step, 0)


def stencil_rows(sz, gx, ny, layers, meta):
    stencil, planes = sz.stencil, 3 * layers
    shape = (TILE, TILE)
    source, lane = iota(shape, 0) - sz.mo, iota(shape, 1)
    dx, dy = (dot(meta, one_hot((source == lane + d * stencil) & (lane < stencil))) for d in range(2))
    ax, ay, az = (dot(meta, one_hot(source == 2 * stencil + d)) for d in range(3))
    layer = jnp.floor((az + 0.5) * (1.0 / TILE))
    line = ((ax + dx) * ny + ay + dy) * planes + layer
    line = jnp.where((dx < 0.5 * DEAD) & (ax > 0.5), line, float(gx * planes * ny))
    return line


def spread_kernel(sz, gx, ny, nyb, layers, parts, begin, end, *refs):
    recv, (expand, table, start), refs = refs[:parts], refs[parts : 3 + parts], refs[3 + parts :]
    grid, rows_out = refs[0], refs[1 : 1 + parts]
    if end:
        keep, send = refs[1 + parts : 3 + parts]
    points, lines, forces, w0, wz0, w1, wz1, terms, rows_s, sem = refs[(3 if end else 1) + parts :]
    slots = points.shape[0]
    planes = 3 * layers
    stencil = sz.stencil
    count = slots // GROUP

    copies = []
    for i, part in enumerate(recv):
        size = part.shape[0]
        meta = part[:, sz.mt : sz.mt + TILE]
        rows_out[i][...] = stencil_rows(sz, gx, ny, layers, meta).astype(jnp.int32)
        copies.append(pltpu.make_async_copy(rows_out[i], rows_s.at[pl.ds(i * size, size)], sem.at[i]))
        copies[-1].start()
    load_records(sz, recv, points, lines)
    base = 0
    for part in recv:
        size = part.shape[0]
        forces[base : base + size] = dot(part[:, 3 * sz.qw :], expand[...])
        base += size
    if begin:
        grid[...] = jnp.zeros(grid.shape, f32)
        size = nyb * planes
        for x in range(gx):
            grid[pl.ds(pl.multiple_of(x * ny * planes + lax.axis_index("batch") * size, 8), size), :] = start[x * size : (x + 1) * size]
    for copy in copies:
        copy.wait()

    def prepare(g, w_ref, wz_ref):
        g = jnp.minimum(g, count - 1)
        line_weights(sz, g, points, lines, w_ref)
        oz = points[pl.ds(pl.multiple_of(g * GROUP, GROUP), GROUP), 2 * sz.qw :]
        left = jnp.transpose(height_factors(oz))
        yield
        for u in range(0, GROUP * TILE, 2 * TILE):
            for t in range(0, sz.qw, TILE):
                exponents = dot(left[t : t + TILE], table[:, u : u + 2 * TILE])
                wz_ref[t : t + TILE, u : u + 2 * TILE] = jnp.exp2(exponents).astype(bf16)
                yield

    def use(g, w_ref, wz_ref):
        first = pl.multiple_of(g * GROUP, GROUP)
        frc = forces[pl.ds(first, GROUP), :]
        for u in range(GROUP):
            w = w_ref[u * stencil : (u + 1) * stencil]
            weighted = [(frc[u : u + 1, k * sz.qw : (k + 1) * sz.qw] * w).astype(bf16) for k in range(3)]
            sums = dot(jnp.concatenate(weighted, axis=0), wz_ref[:, u * TILE : (u + 1) * TILE])
            for k in range(3):
                for j in range(0, stencil, 8):
                    terms[u, pl.ds(4 * j + k, 8, stride=4), :] = sums[k * stencil + j : k * stencil + j + 8]
            yield
            spots = [pl.ds(rows_s[first + u, j], 3, stride=layers) for j in range(stencil)]
            sums = [grid[spots[j], :] + terms[u, 4 * j : 4 * j + 3] for j in range(stencil)]
            for j in range(stencil):
                grid[spots[j], :] = sums[j]

    run_groups(count, prepare, use, ((w0, wz0), (w1, wz1)))

    if end:
        half = ny // 2 * planes
        mine = lax.axis_index("batch") % 2
        for x in range(gx):
            for ref, part in ((keep, mine), (send, 1 - mine)):
                rows = grid[pl.ds(pl.multiple_of((2 * x + part) * half, 8), half), :]
                ref[x * half : (x + 1) * half] = rows.astype(bf16)


def relax(gx, ny, layers, slabs, own, other, drive, state, last):
    planes = 3 * layers
    rows = ny * planes
    half = rows // 2
    pad = (drive.shape[1] - rows) // 2
    wide = gx + 2 * SWEEPS
    edge = jnp.zeros((pad, TILE), f32)
    mine = lax.axis_index("batch") % 2

    def load(p, carry):
        for ref, part in ((own, mine), (other, 1 - mine)):
            values = ref[pl.ds(pl.multiple_of(p * half, 16), half), :].astype(f32)
            drive[p, pl.ds(pl.multiple_of(pad + part * half, 8), half), :] = values
        for ref in (drive, state):
            ref[p, 0:pad] = edge
            ref[p, pad + rows :] = edge
        return carry

    lax.fori_loop(0, wide, load, 0)

    size = 8 * planes
    lane = iota((size, TILE), 1)
    layer = iota((size, TILE), 0) % layers
    last_lane, first_lane = lane == TILE - 1, lane == 0
    above = jnp.where(layer < layers - 1, 1.0, 0.0)
    below = jnp.where(layer > 0, 1.0, 0.0)

    def sweep(source, p, store):
        for at in range(0, rows, size):
            def near(step):
                return source[p, pl.ds(pad + at + step, size), :]

            upper = pltpu.roll(jnp.where(first_lane, near(1) * above, near(0)), TILE - 1, 1)
            lower = pltpu.roll(jnp.where(last_lane, near(-1) * below, near(0)), 1, 1)
            around = source[p - 1, pl.ds(pad + at, size), :] + source[p + 1, pl.ds(pad + at, size), :]
            around = around + near(planes) + near(-planes) + upper + lower
            centre = drive[p, pl.ds(pad + at, size), :]
            store(p, at, (centre + coupling * around) * (1.0 / (1.0 + 6.0 * coupling)))

    def first_sweep(p, carry):
        inside = ((p >= SWEEPS) | (lax.axis_index("slab") > 0)) & ((p < gx + SWEEPS) | (lax.axis_index("slab") < slabs - 1))
        factor = inside.astype(f32)

        def store(p, at, value):
            state[p, pl.ds(pad + at, size), :] = value * factor

        sweep(drive, p, store)
        return carry

    lax.fori_loop(1, wide - 1, first_sweep, 0)

    def second_sweep(p, carry):
        def store(p, at, value):
            last[pl.ds(pl.multiple_of((p - SWEEPS) * rows + at, 8), size), :] = value

        sweep(state, p, store)
        return carry

    lax.fori_loop(SWEEPS, gx + SWEEPS, second_sweep, 0)
    last[gx * rows :] = jnp.zeros((last.shape[0] - gx * rows, TILE), f32)


def sample_kernel(sz, gx, ny, nyb, layers, slabs, parts, begin, *refs):
    lines_in, recv, (expand, table), refs = refs[:parts], refs[parts : 2 * parts], refs[2 * parts : 2 + 2 * parts], refs[2 + 2 * parts :]
    if begin:
        own, other, last, vnew = refs[:4]
        back, (drive, state), refs = refs[4 : 4 + parts], refs[4 + parts : 6 + parts], refs[6 + parts :]
    else:
        last, back, refs = refs[0], refs[1 : 1 + parts], refs[1 + parts :]
    points, lines, w0, wz0, w1, wz1, gathered, products, sampled, rows_s, sem = refs
    copies = []
    for i, part in enumerate(lines_in):
        size = part.shape[0]
        copies.append(pltpu.make_async_copy(part, rows_s.at[pl.ds(i * size, size)], sem.at[i]))
        copies[-1].start()
    stencil = sz.stencil
    slots = points.shape[0]
    count = slots // GROUP
    planes = 3 * layers
    load_records(sz, recv, points, lines)
    if begin:
        relax(gx, ny, layers, slabs, own, other, drive, state, last)
        size = nyb * planes
        for x in range(gx):
            at = pl.multiple_of(x * ny * planes + lax.axis_index("batch") * size, 8)
            vnew[x * size : (x + 1) * size] = last[pl.ds(at, size), :]
    shape = (3 * GROUP, 3 * GROUP * stencil)
    cell, part = iota(shape, 1) // (3 * stencil), iota(shape, 1) // stencil % 3
    adds = one_hot(iota(shape, 0) == part * GROUP + cell)

    for copy in copies:
        copy.wait()
    cut = sz.qw // MXU_LANES * MXU_LANES
    heights = (iota((TILE, TILE), 0).astype(f32) - MIDDLE) * math.sqrt(square)

    def prepare(g, w_ref, wz_ref):
        g = jnp.minimum(g, count - 1)
        line_weights(sz, g, points, lines, w_ref)
        oz = points[pl.ds(pl.multiple_of(g * GROUP, GROUP), GROUP), 2 * sz.qw :]
        right = height_factors(oz[:, :cut]) if cut else None
        rest = oz[:, cut:] * math.sqrt(square)
        yield
        for u in range(GROUP):
            if cut:
                exponents = dot(table[u * TILE : (u + 1) * TILE], right)
                wz_ref[u * TILE : (u + 1) * TILE, :cut] = jnp.exp2(exponents).astype(bf16)
            for t in range(cut, sz.qw, TILE):
                away = rest[u : u + 1, t - cut : t - cut + TILE] - heights
                value = jnp.exp2(norm_bits - away * away).astype(bf16)
                wz_ref[u * TILE : (u + 1) * TILE, t : t + TILE] = value
            yield

    def use(g, w_ref, wz_ref):
        first = pl.multiple_of(g * GROUP, GROUP)
        for u in range(GROUP):
            for j in range(stencil):
                spot = pl.ds(rows_s[first + u, j], 3, stride=layers)
                gathered[u, 4 * j : 4 * j + 3] = last[spot, :]
        for u in range(GROUP):
            tiles = [
                gathered[u, pl.ds(4 * j + k, 8, stride=4), :] for k in range(3) for j in range(0, stencil, 8)
            ]
            projected = dot(jnp.concatenate(tiles, axis=0).astype(bf16), wz_ref[u * TILE : (u + 1) * TILE])
            w = w_ref[u * stencil : (u + 1) * stencil]
            for k in range(3):
                at = (u * 3 + k) * stencil
                products[at : at + stencil] = (projected[k * stencil : (k + 1) * stencil] * w).astype(bf16)
            yield
        values = dot(adds, products[...])
        for k in range(3):
            sampled[pl.ds(first, GROUP), k * sz.qw : (k + 1) * sz.qw] = values[k * GROUP : (k + 1) * GROUP]

    run_groups(count, prepare, use, ((w0, wz0), (w1, wz1)))
    base = 0
    for ref in back:
        size = ref.shape[0]
        ref[...] = dot(sampled[base : base + size].astype(bf16), expand[...], 1, 1).astype(bf16)
        base += size


def unpack_kernel(sz, *refs):
    slot, out = refs[0], refs[-1]
    parts = refs[1:-1]
    cells, size = slot.shape[1], parts[0].shape[0]
    coef = jnp.zeros((cells, sz.cw), f32)
    for c, back in enumerate(parts):
        place = one_hot(slot[...] == iota((size, cells), 0) + c * size)
        coef = coef + dot(place, back[...], 0, 0)
    coef = coef.astype(bf16)
    for k in range(3):
        shape = (sz.terms, sz.cw)
        pick = one_hot(iota(shape, 1) == iota(shape, 0) + k * sz.terms)
        out[k] = dot(pick, coef, 1, 1).astype(bf16)


def local(
    velocity_old, traction, offsets, owner_slab, anchor, blocks, block_count, synthesis, analysis
):
    cells, _, terms = traction.shape
    gx, nyb, layers = velocity_old.shape[:3]
    slabs, batches = lax.axis_size("slab"), lax.axis_size("batch")
    ny = nyb * batches
    planes = 3 * layers
    cap = 2 * cells // slabs
    stencil = blocks.shape[1]
    sz = Sizes(terms, offsets.shape[2], stencil)
    half = ny // 2
    grid_rows = gx * ny * planes + 8 * planes

    pairwise = cap % 16 == 0 and slabs & (slabs - 1) == 0
    if pairwise:
        chunks, size = slabs, cap
        stages = [list(range(min(4, slabs)))] + ([list(range(4, slabs))] if slabs > 4 else [])
        back_stages = [list(range(4, slabs)), list(range(1, min(4, slabs))), [0]]
        back_stages = [stage for stage in back_stages if stage]
    else:
        chunks = next(c for c in (3, 2, 1) if cap % c == 0 and slabs * (cap // c) % 16 == 0)
        size = slabs * cap // chunks
        stages = back_stages = [[c] for c in range(chunks)]

    def exchange(value, p):
        if not pairwise:
            return lax.all_to_all(value, "slab", split_axis=0, concat_axis=0, tiled=True)
        return lax.ppermute(value, "slab", [(i, i ^ p) for i in range(slabs)]) if p else value

    def shape(dims, dtype):
        return jax.ShapeDtypeStruct(dims, dtype)

    def whole(dims):
        return pl.BlockSpec(dims, lambda i: (0,) * len(dims))

    packed = [
        owner_slab.T,
        anchor.T,
        blocks.T,
        block_count.reshape(1, cells),
        traction.transpose(1, 2, 0),
        offsets.transpose(1, 0, 2),
    ]
    send = pl.pallas_call(
        lambda *refs: pack_kernel(sz, slabs, cap, chunks, pairwise, ny, layers, *refs),
        grid=(1,),
        out_shape=[shape((size, sz.width), bf16)] * chunks + [shape((1, cells), jnp.int32)],
        in_specs=[whole(value.shape) for value in packed],
        out_specs=[whole((size, sz.width))] * chunks + [whole((1, cells))],
        scratch_shapes=[pltpu.VMEM((cells, sz.width), bf16)],
        compiler_params=pltpu.CompilerParams(vmem_limit_bytes=60 * 1024 * 1024),
        name="pack",
    )(*packed)
    slot = send[chunks]
    recv = [exchange(send[p], p) for p in range(chunks)]

    expand_shape = shape((sz.cw, 3 * sz.qw), bf16)
    spread_basis, sample_basis, spread_table, sample_table = pl.pallas_call(
        lambda *refs: basis_kernel(sz, *refs),
        out_shape=[expand_shape, expand_shape, shape((TILE, GROUP * TILE), bf16), shape((GROUP * TILE, TILE), bf16)],
        in_specs=vmem(2),
        out_specs=vmem(4),
        compiler_params=params,
        name="basis",
    )(synthesis, analysis)

    grid_shape = shape((grid_rows, TILE), f32)
    half_shape = shape((gx * planes * half, TILE), bf16)
    weights_xy = pltpu.VMEM((GROUP * stencil, sz.qw), f32)
    terms_shape = pltpu.VMEM((GROUP, 4 * stencil, TILE), f32)
    grid = velocity_old.transpose(0, 1, 3, 2, 4).reshape(-1, TILE)
    rows = {}
    for stage in stages:
        parts = len(stage)
        slots = parts * size
        begin, end = stage is stages[0], stage is stages[-1]
        points = [pltpu.VMEM((slots, 3 * sz.qw), f32), pltpu.VMEM((2, slots // GROUP, TILE), f32)]
        out = pl.pallas_call(
            lambda *refs: spread_kernel(sz, gx, ny, nyb, layers, parts, begin, end, *refs),
            out_shape=[
                grid_shape,
            ]
            + [shape((size, TILE), jnp.int32)] * parts
            + [half_shape] * (2 * end),
            in_specs=vmem(parts + 3),
            out_specs=vmem(1 + parts + 2 * end),
            scratch_shapes=points
            + [pltpu.VMEM((slots, 3 * sz.qw), f32)]
            + [weights_xy, pltpu.VMEM((sz.qw, GROUP * TILE), bf16)] * 2
            + [terms_shape, pltpu.SMEM((slots, TILE), jnp.int32), pltpu.SemaphoreType.DMA((parts,))],
            input_output_aliases={} if begin else {2 + parts: 0},
            compiler_params=params,
            cost_estimate=pl.CostEstimate(flops=100_000_000 * slots, bytes_accessed=4_000_000, transcendentals=0),
            name="spread",
        )(*(recv[p] for p in stage), spread_basis, spread_table, grid)
        grid = out[0]
        rows.update(zip(stage, out[1 : 1 + parts]))
    keep, send_half = out[-2:]

    def pairs(bit):
        return [(i, i ^ bit) for i in range(batches)]

    def add(a, b):
        return (a.astype(f32) + b.astype(f32)).astype(bf16)

    mine = add(keep, lax.ppermute(send_half, "batch", pairs(1)))
    halo = SWEEPS * planes * half
    low = lax.ppermute(mine[-halo:], "slab", [(i, i + 1) for i in range(slabs - 1)])
    high = lax.ppermute(mine[:halo], "slab", [(i + 1, i) for i in range(slabs - 1)])
    edges = jnp.concatenate([low, high], axis=0)
    bit = 2
    while bit < batches:
        got = lax.ppermute(mine, "batch", pairs(bit))
        edges, got = lax.optimization_barrier((edges, got))
        mine = add(mine, got)
        edges = add(edges, lax.ppermute(edges, "batch", pairs(bit)))
        bit *= 2
    mine = jnp.concatenate([edges[:halo], mine, edges[halo:]], axis=0)
    other = lax.ppermute(mine, "batch", pairs(1))

    wide = gx + 2 * SWEEPS
    padded = pltpu.VMEM((wide, planes * ny + 16, TILE), f32)
    returned = [None] * chunks
    for stage in back_stages:
        parts = len(stage)
        slots = parts * size
        begin = stage is back_stages[0]
        out = pl.pallas_call(
            lambda *refs: sample_kernel(sz, gx, ny, nyb, layers, slabs, parts, begin, *refs),
            out_shape=([grid_shape, shape((gx * nyb * planes, TILE), f32)] if begin else [])
            + [shape((size, sz.cw), bf16)] * parts,
            in_specs=vmem(2 * parts + 2) + vmem(2 if begin else 1),
            out_specs=vmem(2 * begin + parts),
            scratch_shapes=([padded, padded] if begin else [])
            + [pltpu.VMEM((slots, 3 * sz.qw), f32), pltpu.VMEM((2, slots // GROUP, TILE), f32)]
            + [weights_xy, pltpu.VMEM((GROUP * TILE, sz.qw), bf16)] * 2
            + [terms_shape]
            + [pltpu.VMEM((3 * GROUP * stencil, sz.qw), bf16), pltpu.VMEM((slots, 3 * sz.qw), f32)]
            + [pltpu.SMEM((slots, TILE), jnp.int32), pltpu.SemaphoreType.DMA((parts,))],
            compiler_params=params,
            cost_estimate=pl.CostEstimate(flops=50_000_000 * slots, bytes_accessed=4_000_000, transcendentals=0),
            name="sample",
        )(*(rows[p] for p in stage), *(recv[p] for p in stage), sample_basis, sample_table, *((mine, other) if begin else (grid,)))
        if begin:
            grid, vnew = out[:2]
        for p, back in zip(stage, out[2 * begin :]):
            returned[p] = exchange(back, p)
    velocity_new = vnew.reshape(gx, nyb, 3, layers, TILE).transpose(0, 1, 3, 2, 4)

    coef = pl.pallas_call(
        lambda *refs: unpack_kernel(sz, *refs),
        out_shape=shape((3, terms, cells), bf16),
        in_specs=vmem(1 + chunks),
        out_specs=vmem(1)[0],
        compiler_params=params,
        name="unpack",
    )(slot, *returned)
    return velocity_new, coef.transpose(2, 0, 1)


def solution(mesh):
    in_specs = (
        P("slab", "batch", None, None, None),
        P(("slab", "batch"), None, None),
        P(("slab", "batch"), None, None),
        P(("slab", "batch"), None),
        P(("slab", "batch"), None),
        P(("slab", "batch"), None),
        P(("slab", "batch")),
        P(),
        P(),
    )
    out_specs = (P("slab", "batch", None, None, None), P(("slab", "batch"), None, None))
    return jax.shard_map(local, mesh=mesh, in_specs=in_specs, out_specs=out_specs, check_vma=False)
```

```python
import math

import jax
import jax.numpy as jnp
from jax import lax
from jax.experimental import pallas as pl
from jax.experimental.pallas import tpu as pltpu
from jax.sharding import PartitionSpec as P

SWEEPS = 2
TILE = 128
GROUP = 8
MXU_LANES = 256
UNROLL = 12
DEAD = 64.0
MIDDLE = 64.0

kernel_width = 0.8
kernel_norm = 1.0 / (0.8 * math.sqrt(2.0 * math.pi))
coupling = 2.0
square = 0.5 / (math.log(2.0) * kernel_width * kernel_width)
norm_bits = math.log2(kernel_norm)

f32 = jnp.float32
bf16 = jnp.bfloat16


def round_up(value, step):
    return -(-value // step) * step


def iota(shape, dim):
    return lax.broadcasted_iota(jnp.int32, shape, dim)


def one_hot(mask):
    return jnp.where(mask, 1.0, 0.0).astype(bf16)


def dot(a, b, ca=1, cb=0):
    return lax.dot_general(a, b, (((ca,), (cb,)), ((), ())), preferred_element_type=f32)


def vmem(count=1):
    return [pl.BlockSpec(memory_space=pltpu.VMEM)] * count


params = pltpu.CompilerParams(vmem_limit_bytes=12 * 1024 * 1024)


class Sizes:
    def __init__(self, terms, points, stencil):
        self.terms, self.points, self.stencil = terms, points, stencil
        self.qw = round_up(points, TILE)
        self.cw = round_up(3 * terms, TILE)
        self.width = 3 * self.qw + self.cw
        self.mt = points // TILE * TILE
        self.mo = points - self.mt
        self.meta = 2 * stencil + 3
        self.rows = round_up(self.meta, 8)


def place_terms(sz, k):
    shape = (sz.cw, sz.terms)
    return one_hot(iota(shape, 0) == iota(shape, 1) + k * sz.terms)


def pieces(value, count):
    out = []
    for _ in range(count):
        part = value.astype(bf16).astype(f32)
        out.append(part)
        value = value - part
    return out


def pack_kernel(sz, slabs, cap, chunks, pairwise, ny, layers, *refs):
    owner, anchor, blocks, count, trac, offs = refs[:6]
    send, slot_out, rec = refs[6 : 6 + chunks], refs[6 + chunks], refs[7 + chunks]
    cells = owner.shape[1]
    slots = slabs * cap
    own = owner[...]
    member = one_hot(own == iota((slabs, cells), 0))
    before = one_hot(iota((cells, cells), 0) < iota((cells, cells), 1))
    rank = jnp.sum(member.astype(f32) * dot(member, before), axis=0, keepdims=True)
    if pairwise:
        slot = (own ^ lax.axis_index("slab")) * cap + rank.astype(jnp.int32)
    else:
        part = cap // chunks
        chunk = jnp.floor((rank + 0.5) * (1.0 / part))
        slot = (chunk * (slabs * part - part) + rank).astype(jnp.int32) + own * part
    slot_out[...] = slot
    place = one_hot(slot == iota((slots, cells), 0))

    tile = blocks[...].astype(f32)
    anchors = anchor[...].astype(f32)
    tile_x = jnp.floor((tile + 0.5) * (1.0 / (ny * layers)))
    tile_y = jnp.floor((tile + 0.5) * (1.0 / layers)) - tile_x * ny
    live = iota(tile.shape, 0) < count[...]
    dx = jnp.where(live, tile_x - anchors[0:1], DEAD)
    dy = jnp.where(live, tile_y - anchors[1:2], DEAD)

    rec[...] = jnp.zeros(rec.shape, bf16)
    for k in range(3):
        rec[:, k * sz.qw : k * sz.qw + sz.points] = offs[k]
    base = sz.mo
    meta = jnp.zeros((cells, TILE), f32)
    for row in (dx, dy, anchors):
        shape = (row.shape[0], TILE)
        where = one_hot(iota(shape, 1) == iota(shape, 0) + base)
        meta = meta + dot(row.astype(bf16), where, 0, 0)
        base += row.shape[0]
    rec[:, sz.mt : sz.mt + TILE] = rec[:, sz.mt : sz.mt + TILE] + meta.astype(bf16)
    coef = jnp.zeros((cells, sz.cw), f32)
    for k in range(3):
        coef = coef + dot(trac[k], place_terms(sz, k), 0, 1)
    rec[:, 3 * sz.qw :] = coef.astype(bf16)
    size = slots // chunks
    for c in range(chunks):
        send[c][...] = dot(place[c * size : (c + 1) * size], rec[...]).astype(bf16)


def load_records(sz, recv, points, lines):
    stencil = sz.stencil
    base = 0
    shape = (TILE, TILE)
    for part in recv:
        slots = part.shape[0]
        points[base : base + slots] = part[:, : 3 * sz.qw].astype(f32)
        meta = part[:, sz.mt : sz.mt + TILE]
        az = dot(meta, one_hot(iota(shape, 0) == sz.mo + 2 * stencil + 2))
        height = az - TILE * jnp.floor((az + 0.5) * (1.0 / TILE)) - MIDDLE
        for t in range(2 * sz.qw, 3 * sz.qw, TILE):
            points[base : base + slots, t : t + TILE] = points[base : base + slots, t : t + TILE] + height
        groups = slots // GROUP
        merge = one_hot(iota((groups, slots), 0) == iota((groups, slots), 1) // GROUP)
        mine = iota((slots, TILE), 0) % GROUP == iota((slots, TILE), 1) // stencil
        for d in range(2):
            spread = one_hot(iota(shape, 0) == iota(shape, 1) % stencil + sz.mo + d * stencil)
            lines[d, base // GROUP : base // GROUP + groups] = dot(
                merge, jnp.where(mine, dot(meta, spread), 0.0).astype(bf16)
            )
        base += slots


def height_table(shape, dim):
    cell, height = iota(shape, dim) // TILE, iota(shape, dim) % TILE
    kind, mine = iota(shape, 1 - dim) // GROUP, iota(shape, 1 - dim) % GROUP == cell
    m = height.astype(f32) - MIDDLE
    minus = pieces(-square * m * m, 3)
    value = jnp.where(kind < 3, m, jnp.where(kind < 6, 1.0, 0.0))
    for i in range(3):
        value = jnp.where(kind == 6 + i, minus[i], value)
    return jnp.where(mine, value, 0.0).astype(bf16)


def stack_rows(rows, like):
    rows = rows + [jnp.zeros_like(like)] * (TILE // GROUP - len(rows))
    return jnp.concatenate(rows, axis=0).astype(bf16)


def line_weights(sz, g, points, lines, w_ref):
    first = pl.multiple_of(g * GROUP, GROUP)
    pts = points[pl.ds(first, GROUP), : 2 * sz.qw]
    ox, oy = pts[:, : sz.qw], pts[:, sz.qw :]
    steps = [lines[d, pl.ds(g, 1), :] for d in range(2)]
    mine = iota((GROUP, TILE), 0) == iota((GROUP, TILE), 1) // sz.stencil
    dx, dy, norm = (jnp.where(mine, value, 0.0) for value in (*steps, steps[0] * steps[0] + steps[1] * steps[1]))
    unit = jnp.where(mine, 1.0, 0.0)
    left = stack_rows([dx, dx, dy, dy, unit, unit, norm, norm], dx)
    rows = pieces(2.0 * square * ox, 2) + pieces(2.0 * square * oy, 2)
    rows = rows + pieces(2.0 * norm_bits - square * (ox * ox + oy * oy), 2)
    rows = rows + pieces(jnp.full_like(ox, -square), 2)
    w_ref[...] = jnp.exp2(dot(left, stack_rows(rows, ox), 0, 0))


def height_factors(oz):
    rows = pieces(2.0 * square * oz, 3) + pieces(norm_bits - square * oz * oz, 3) + [jnp.ones_like(oz)] * 3
    return stack_rows(rows, oz)


def basis_kernel(sz, dim, basis, out, table):
    out[...] = jnp.zeros(out.shape, bf16)
    for k in range(3):
        out[:, k * sz.qw : k * sz.qw + sz.points] = dot(place_terms(sz, k), basis[...]).astype(bf16)
    table[...] = height_table(table.shape, dim)


def in_turn(*works):
    works = list(works)
    while works:
        works = [work for work in works if next(work, works) is not works]


def run_groups(count, prepare, use, slots):
    in_turn(prepare(0, *slots[0]))
    turns = next(t for t in (UNROLL, 6, 4, 2, 1) if count % t == 0)

    def step(h, carry):
        for i in range(turns):
            g = turns * h + i
            if turns % 2:
                in_turn(use(g, *slots[0]))
                in_turn(prepare(g + 1, *slots[0]))
            else:
                in_turn(prepare(g + 1, *slots[(i + 1) % 2]), use(g, *slots[i % 2]))
        return carry

    lax.fori_loop(0, count // turns, step, 0)


def stencil_rows(sz, gx, ny, layers, meta):
    stencil, planes = sz.stencil, 3 * layers
    shape = (TILE, TILE)
    source, lane = iota(shape, 0) - sz.mo, iota(shape, 1)
    dx, dy = (dot(meta, one_hot((source == lane + d * stencil) & (lane < stencil))) for d in range(2))
    ax, ay, az = (dot(meta, one_hot(source == 2 * stencil + d)) for d in range(3))
    layer = jnp.floor((az + 0.5) * (1.0 / TILE))
    line = ((ax + dx) * ny + ay + dy) * planes + layer
    line = jnp.where((dx < 0.5 * DEAD) & (ax > 0.5), line, float(gx * planes * ny))
    return line


def spread_kernel(sz, gx, ny, nyb, layers, parts, begin, end, *refs):
    recv, (expand, table, start), refs = refs[:parts], refs[parts : 3 + parts], refs[3 + parts :]
    grid, rows_out = refs[0], refs[1 : 1 + parts]
    if end:
        keep, send = refs[1 + parts : 3 + parts]
    points, lines, forces, w0, wz0, w1, wz1, terms, rows_s, sem = refs[(3 if end else 1) + parts :]
    slots = points.shape[0]
    planes = 3 * layers
    stencil = sz.stencil
    count = slots // GROUP

    copies = []
    for i, part in enumerate(recv):
        size = part.shape[0]
        meta = part[:, sz.mt : sz.mt + TILE]
        rows_out[i][...] = stencil_rows(sz, gx, ny, layers, meta).astype(jnp.int32)
        copies.append(pltpu.make_async_copy(rows_out[i], rows_s.at[pl.ds(i * size, size)], sem.at[i]))
        copies[-1].start()
    load_records(sz, recv, points, lines)
    base = 0
    for part in recv:
        size = part.shape[0]
        forces[base : base + size] = dot(part[:, 3 * sz.qw :], expand[...])
        base += size
    if begin:
        grid[...] = jnp.zeros(grid.shape, f32)
        size = nyb * planes
        for x in range(gx):
            grid[pl.ds(pl.multiple_of(x * ny * planes + lax.axis_index("batch") * size, 8), size), :] = start[x * size : (x + 1) * size]
    for copy in copies:
        copy.wait()

    def prepare(g, w_ref, wz_ref):
        g = jnp.minimum(g, count - 1)
        line_weights(sz, g, points, lines, w_ref)
        oz = points[pl.ds(pl.multiple_of(g * GROUP, GROUP), GROUP), 2 * sz.qw :]
        left = jnp.transpose(height_factors(oz))
        yield
        for u in range(0, GROUP * TILE, 2 * TILE):
            for t in range(0, sz.qw, TILE):
                exponents = dot(left[t : t + TILE], table[:, u : u + 2 * TILE])
                wz_ref[t : t + TILE, u : u + 2 * TILE] = jnp.exp2(exponents).astype(bf16)
                yield

    def use(g, w_ref, wz_ref):
        first = pl.multiple_of(g * GROUP, GROUP)
        frc = forces[pl.ds(first, GROUP), :]
        for u in range(GROUP):
            w = w_ref[u * stencil : (u + 1) * stencil]
            weighted = [(frc[u : u + 1, k * sz.qw : (k + 1) * sz.qw] * w).astype(bf16) for k in range(3)]
            sums = dot(jnp.concatenate(weighted, axis=0), wz_ref[:, u * TILE : (u + 1) * TILE])
            for k in range(3):
                for j in range(0, stencil, 8):
                    terms[u, pl.ds(4 * j + k, 8, stride=4), :] = sums[k * stencil + j : k * stencil + j + 8]
            yield
            spots = [pl.ds(rows_s[first + u, j], 3, stride=layers) for j in range(stencil)]
            sums = [grid[spots[j], :] + terms[u, 4 * j : 4 * j + 3] for j in range(stencil)]
            for j in range(stencil):
                grid[spots[j], :] = sums[j]

    run_groups(count, prepare, use, ((w0, wz0), (w1, wz1)))

    if end:
        half = ny // 2 * planes
        mine = lax.axis_index("batch") % 2
        for x in range(gx):
            for ref, part in ((keep, mine), (send, 1 - mine)):
                rows = grid[pl.ds(pl.multiple_of((2 * x + part) * half, 8), half), :]
                ref[x * half : (x + 1) * half] = rows.astype(bf16)


def relax(gx, ny, layers, slabs, own, other, drive, state, last):
    planes = 3 * layers
    rows = ny * planes
    half = rows // 2
    pad = (drive.shape[1] - rows) // 2
    wide = gx + 2 * SWEEPS
    edge = jnp.zeros((pad, TILE), f32)
    mine = lax.axis_index("batch") % 2

    def load(p, carry):
        for ref, part in ((own, mine), (other, 1 - mine)):
            values = ref[pl.ds(pl.multiple_of(p * half, 16), half), :].astype(f32)
            drive[p, pl.ds(pl.multiple_of(pad + part * half, 8), half), :] = values
        for ref in (drive, state):
            ref[p, 0:pad] = edge
            ref[p, pad + rows :] = edge
        return carry

    lax.fori_loop(0, wide, load, 0)

    size = 8 * planes
    lane = iota((size, TILE), 1)
    layer = iota((size, TILE), 0) % layers
    last_lane, first_lane = lane == TILE - 1, lane == 0
    above = jnp.where(layer < layers - 1, 1.0, 0.0)
    below = jnp.where(layer > 0, 1.0, 0.0)

    def sweep(source, p, store):
        for at in range(0, rows, size):
            def near(step):
                return source[p, pl.ds(pad + at + step, size), :]

            upper = pltpu.roll(jnp.where(first_lane, near(1) * above, near(0)), TILE - 1, 1)
            lower = pltpu.roll(jnp.where(last_lane, near(-1) * below, near(0)), 1, 1)
            around = source[p - 1, pl.ds(pad + at, size), :] + source[p + 1, pl.ds(pad + at, size), :]
            around = around + near(planes) + near(-planes) + upper + lower
            centre = drive[p, pl.ds(pad + at, size), :]
            store(p, at, (centre + coupling * around) * (1.0 / (1.0 + 6.0 * coupling)))

    def first_sweep(p, carry):
        inside = ((p >= SWEEPS) | (lax.axis_index("slab") > 0)) & ((p < gx + SWEEPS) | (lax.axis_index("slab") < slabs - 1))
        factor = inside.astype(f32)

        def store(p, at, value):
            state[p, pl.ds(pad + at, size), :] = value * factor

        sweep(drive, p, store)
        return carry

    lax.fori_loop(1, wide - 1, first_sweep, 0)

    def second_sweep(p, carry):
        def store(p, at, value):
            last[pl.ds(pl.multiple_of((p - SWEEPS) * rows + at, 8), size), :] = value

        sweep(state, p, store)
        return carry

    lax.fori_loop(SWEEPS, gx + SWEEPS, second_sweep, 0)
    last[gx * rows :] = jnp.zeros((last.shape[0] - gx * rows, TILE), f32)


def sample_weights(sz, g, points, lines, table, w_ref, wz_ref):
    cut = sz.qw // MXU_LANES * MXU_LANES
    heights = (iota((TILE, TILE), 0).astype(f32) - MIDDLE) * math.sqrt(square)
    line_weights(sz, g, points, lines, w_ref)
    oz = points[pl.ds(pl.multiple_of(g * GROUP, GROUP), GROUP), 2 * sz.qw :]
    right = height_factors(oz[:, :cut]) if cut else None
    rest = oz[:, cut:] * math.sqrt(square)
    yield
    for u in range(GROUP):
        if cut:
            exponents = dot(table[u * TILE : (u + 1) * TILE], right)
            wz_ref[u * TILE : (u + 1) * TILE, :cut] = jnp.exp2(exponents).astype(bf16)
        for t in range(cut, sz.qw, TILE):
            away = rest[u : u + 1, t - cut : t - cut + TILE] - heights
            value = jnp.exp2(norm_bits - away * away).astype(bf16)
            wz_ref[u * TILE : (u + 1) * TILE, t : t + TILE] = value
        yield


def weights_kernel(sz, parts, *refs):
    recv, (table, w_out, wz_out, points, lines) = refs[:parts], refs[parts:]
    load_records(sz, recv, points, lines)
    count = w_out.shape[0]
    turns = next(t for t in (4, 2, 1) if count % t == 0)

    def step(h, carry):
        groups = [turns * h + i for i in range(turns)]
        for g in groups:
            in_turn(sample_weights(sz, g, points, lines, table, w_out.at[g], wz_out.at[g]))
        return carry

    lax.fori_loop(0, count // turns, step, 0)


def sample_kernel(sz, gx, ny, nyb, layers, slabs, parts, begin, halves, *refs):
    lines_in, refs = refs[:parts], refs[parts:]
    if begin:
        ready, refs = refs[: 2 * halves], refs[2 * halves :]
        expand, own, other, last, vnew = refs[:5]
        back, (drive, state, *refs) = refs[5 : 5 + parts], refs[5 + parts :]
    else:
        recv, (expand, table, last), refs = refs[:parts], refs[parts : 3 + parts], refs[3 + parts :]
        back, (points, lines, w0, wz0, w1, wz1, *refs) = refs[:parts], refs[parts:]
    gathered, products, sampled, rows_s, sem = refs
    copies = []
    for i, part in enumerate(lines_in):
        size = part.shape[0]
        copies.append(pltpu.make_async_copy(part, rows_s.at[pl.ds(i * size, size)], sem.at[i]))
        copies[-1].start()
    stencil = sz.stencil
    slots = sampled.shape[0]
    count = slots // GROUP
    planes = 3 * layers
    if not begin:
        load_records(sz, recv, points, lines)
    else:
        relax(gx, ny, layers, slabs, own, other, drive, state, last)
        size = nyb * planes
        for x in range(gx):
            at = pl.multiple_of(x * ny * planes + lax.axis_index("batch") * size, 8)
            vnew[x * size : (x + 1) * size] = last[pl.ds(at, size), :]
    shape = (3 * GROUP, 3 * GROUP * stencil)
    cell, part = iota(shape, 1) // (3 * stencil), iota(shape, 1) // stencil % 3
    adds = one_hot(iota(shape, 0) == part * GROUP + cell)

    for copy in copies:
        copy.wait()
    def prepare(g, w_ref, wz_ref):
        yield from sample_weights(sz, jnp.minimum(g, count - 1), points, lines, table, w_ref, wz_ref)

    def use(g, w_ref, wz_ref):
        first = pl.multiple_of(g * GROUP, GROUP)
        for u in range(GROUP):
            for j in range(stencil):
                spot = pl.ds(rows_s[first + u, j], 3, stride=layers)
                gathered[u, 4 * j : 4 * j + 3] = last[spot, :]
        for u in range(GROUP):
            tiles = [
                gathered[u, pl.ds(4 * j + k, 8, stride=4), :] for k in range(3) for j in range(0, stencil, 8)
            ]
            projected = dot(jnp.concatenate(tiles, axis=0).astype(bf16), wz_ref[u * TILE : (u + 1) * TILE])
            w = w_ref[u * stencil : (u + 1) * stencil]
            for k in range(3):
                at = (u * 3 + k) * stencil
                products[at : at + stencil] = (projected[k * stencil : (k + 1) * stencil] * w).astype(bf16)
            yield
        values = dot(adds, products[...])
        for k in range(3):
            sampled[pl.ds(first, GROUP), k * sz.qw : (k + 1) * sz.qw] = values[k * GROUP : (k + 1) * GROUP]

    def use_ready(base, w_in, wz_in):
        turns = next(t for t in (UNROLL, 6, 4, 2, 1) if w_in.shape[0] % t == 0)

        def step(h, carry):
            for i in range(turns):
                g = turns * h + i
                in_turn(use(base + g, w_in.at[g], wz_in.at[g]))
            return carry

        lax.fori_loop(0, w_in.shape[0] // turns, step, 0)

    if begin:
        base = 0
        for w_in, wz_in in zip(ready[::2], ready[1::2]):
            use_ready(base, w_in, wz_in)
            base += w_in.shape[0]
    else:
        run_groups(count, prepare, use, ((w0, wz0), (w1, wz1)))
    base = 0
    for ref in back:
        size = ref.shape[0]
        ref[...] = dot(sampled[base : base + size].astype(bf16), expand[...], 1, 1).astype(bf16)
        base += size


def unpack_kernel(sz, *refs):
    slot, out = refs[0], refs[-1]
    parts = refs[1:-1]
    cells, size = slot.shape[1], parts[0].shape[0]
    coef = jnp.zeros((cells, sz.cw), f32)
    for c, back in enumerate(parts):
        place = one_hot(slot[...] == iota((size, cells), 0) + c * size)
        coef = coef + dot(place, back[...], 0, 0)
    coef = coef.astype(bf16)
    for k in range(3):
        shape = (sz.terms, sz.cw)
        pick = one_hot(iota(shape, 1) == iota(shape, 0) + k * sz.terms)
        out[k] = dot(pick, coef, 1, 1).astype(bf16)


def local(
    velocity_old, traction, offsets, owner_slab, anchor, blocks, block_count, synthesis, analysis
):
    cells, _, terms = traction.shape
    gx, nyb, layers = velocity_old.shape[:3]
    slabs, batches = lax.axis_size("slab"), lax.axis_size("batch")
    ny = nyb * batches
    planes = 3 * layers
    cap = 2 * cells // slabs
    stencil = blocks.shape[1]
    sz = Sizes(terms, offsets.shape[2], stencil)
    half = ny // 2
    grid_rows = gx * ny * planes + 8 * planes

    pairwise = cap % 16 == 0 and slabs & (slabs - 1) == 0
    if pairwise:
        chunks, size = slabs, cap
        stages = [list(range(min(4, slabs)))] + ([list(range(4, slabs))] if slabs > 4 else [])
        back_stages = [list(range(4, slabs)), list(range(1, min(4, slabs))), [0]]
        back_stages = [stage for stage in back_stages if stage]
    else:
        chunks = next(c for c in (3, 2, 1) if cap % c == 0 and slabs * (cap // c) % 16 == 0)
        size = slabs * cap // chunks
        stages = back_stages = [[c] for c in range(chunks)]

    def exchange(value, p):
        if not pairwise:
            return lax.all_to_all(value, "slab", split_axis=0, concat_axis=0, tiled=True)
        return lax.ppermute(value, "slab", [(i, i ^ p) for i in range(slabs)]) if p else value

    def shape(dims, dtype):
        return jax.ShapeDtypeStruct(dims, dtype)

    def whole(dims):
        return pl.BlockSpec(dims, lambda i: (0,) * len(dims))

    packed = [
        owner_slab.T,
        anchor.T,
        blocks.T,
        block_count.reshape(1, cells),
        traction.transpose(1, 2, 0),
        offsets.transpose(1, 0, 2),
    ]
    send = pl.pallas_call(
        lambda *refs: pack_kernel(sz, slabs, cap, chunks, pairwise, ny, layers, *refs),
        grid=(1,),
        out_shape=[shape((size, sz.width), bf16)] * chunks + [shape((1, cells), jnp.int32)],
        in_specs=[whole(value.shape) for value in packed],
        out_specs=[whole((size, sz.width))] * chunks + [whole((1, cells))],
        scratch_shapes=[pltpu.VMEM((cells, sz.width), bf16)],
        compiler_params=pltpu.CompilerParams(vmem_limit_bytes=60 * 1024 * 1024),
        name="pack",
    )(*packed)
    slot = send[chunks]
    recv = [exchange(send[p], p) for p in range(chunks)]

    expand_shape = shape((sz.cw, 3 * sz.qw), bf16)
    def basis(values, dim):
        table = (TILE, GROUP * TILE) if dim else (GROUP * TILE, TILE)
        return pl.pallas_call(
            lambda *refs: basis_kernel(sz, dim, *refs),
            out_shape=[expand_shape, shape(table, bf16)],
            in_specs=vmem(1),
            out_specs=vmem(2),
            compiler_params=params,
            name="basis",
        )(values)

    spread_basis, spread_table = basis(synthesis, 1)

    grid_shape = shape((grid_rows, TILE), f32)
    half_shape = shape((gx * planes * half, TILE), bf16)
    weights_xy = pltpu.VMEM((GROUP * stencil, sz.qw), f32)
    terms_shape = pltpu.VMEM((GROUP, 4 * stencil, TILE), f32)
    grid = velocity_old.transpose(0, 1, 3, 2, 4).reshape(-1, TILE)
    rows = {}
    for stage in stages:
        parts = len(stage)
        slots = parts * size
        begin, end = stage is stages[0], stage is stages[-1]
        points = [pltpu.VMEM((slots, 3 * sz.qw), f32), pltpu.VMEM((2, slots // GROUP, TILE), f32)]
        out = pl.pallas_call(
            lambda *refs: spread_kernel(sz, gx, ny, nyb, layers, parts, begin, end, *refs),
            out_shape=[
                grid_shape,
            ]
            + [shape((size, TILE), jnp.int32)] * parts
            + [half_shape] * (2 * end),
            in_specs=vmem(parts + 3),
            out_specs=vmem(1 + parts + 2 * end),
            scratch_shapes=points
            + [pltpu.VMEM((slots, 3 * sz.qw), f32)]
            + [weights_xy, pltpu.VMEM((sz.qw, GROUP * TILE), bf16)] * 2
            + [terms_shape, pltpu.SMEM((slots, TILE), jnp.int32), pltpu.SemaphoreType.DMA((parts,))],
            input_output_aliases={} if begin else {2 + parts: 0},
            compiler_params=params,
            cost_estimate=pl.CostEstimate(flops=100_000_000 * slots, bytes_accessed=4_000_000, transcendentals=0),
            name="spread",
        )(*(recv[p] for p in stage), spread_basis, spread_table, grid)
        grid = out[0]
        rows.update(zip(stage, out[1 : 1 + parts]))
    keep, send_half = out[-2:]

    def pairs(bit):
        return [(i, i ^ bit) for i in range(batches)]

    def add(a, b):
        return (a.astype(f32) + b.astype(f32)).astype(bf16)

    mine = add(keep, lax.ppermute(send_half, "batch", pairs(1)))
    def weights(values):
        slots = len(values) * size
        groups = slots // GROUP
        return pl.pallas_call(
            lambda *refs: weights_kernel(sz, len(values), *refs),
            out_shape=[
                shape((groups, GROUP * stencil, sz.qw), f32),
                shape((groups, GROUP * TILE, sz.qw), bf16),
            ],
            in_specs=vmem(len(values) + 1),
            out_specs=vmem(2),
            scratch_shapes=[pltpu.VMEM((slots, 3 * sz.qw), f32), pltpu.VMEM((2, groups, TILE), f32)],
            compiler_params=params,
            cost_estimate=pl.CostEstimate(flops=50_000_000 * slots, bytes_accessed=4_000_000, transcendentals=0),
            name="weights",
        )(*values, sample_table)

    first = back_stages[0]
    late = [recv[p] for p in first]
    mine, analysis, late = lax.optimization_barrier((mine, analysis, late))
    sample_basis, sample_table = basis(analysis, 0)
    ready = [weights(late[: (len(late) + 1) // 2])]
    halo = SWEEPS * planes * half
    low = lax.ppermute(mine[-halo:], "slab", [(i, i + 1) for i in range(slabs - 1)])
    high = lax.ppermute(mine[:halo], "slab", [(i + 1, i) for i in range(slabs - 1)])
    edges = jnp.concatenate([low, high], axis=0)
    bit = 2
    while bit < batches:
        got = lax.ppermute(mine, "batch", pairs(bit))
        edges, got, ready, late = lax.optimization_barrier((edges, got, ready, late))
        mine = add(mine, got)
        edges = add(edges, lax.ppermute(edges, "batch", pairs(bit)))
        bit *= 2
    mine = jnp.concatenate([edges[:halo], mine, edges[halo:]], axis=0)
    if len(late) > 1:
        ready.append(weights(late[(len(late) + 1) // 2 :]))
        mine, ready = lax.optimization_barrier((mine, ready))
    other = lax.ppermute(mine, "batch", pairs(1))

    wide = gx + 2 * SWEEPS
    padded = pltpu.VMEM((wide, planes * ny + 16, TILE), f32)
    returned = [None] * chunks
    for stage in back_stages:
        parts = len(stage)
        slots = parts * size
        begin = stage is back_stages[0]
        out = pl.pallas_call(
            lambda *refs: sample_kernel(sz, gx, ny, nyb, layers, slabs, parts, begin, len(ready), *refs),
            out_shape=([grid_shape, shape((gx * nyb * planes, TILE), f32)] if begin else [])
            + [shape((size, sz.cw), bf16)] * parts,
            in_specs=vmem(parts + 2 * len(ready) + 3 if begin else 2 * parts + 3),
            out_specs=vmem(2 * begin + parts),
            scratch_shapes=(
                [padded, padded]
                if begin
                else [pltpu.VMEM((slots, 3 * sz.qw), f32), pltpu.VMEM((2, slots // GROUP, TILE), f32)]
                + [weights_xy, pltpu.VMEM((GROUP * TILE, sz.qw), bf16)] * 2
            )
            + [terms_shape]
            + [pltpu.VMEM((3 * GROUP * stencil, sz.qw), bf16), pltpu.VMEM((slots, 3 * sz.qw), f32)]
            + [pltpu.SMEM((slots, TILE), jnp.int32), pltpu.SemaphoreType.DMA((parts,))],
            compiler_params=params,
            cost_estimate=pl.CostEstimate(flops=50_000_000 * slots, bytes_accessed=4_000_000, transcendentals=0),
            name="sample",
        )(
            *(rows[p] for p in stage),
            *((*sum(map(list, ready), []), sample_basis, mine, other) if begin else (*(recv[p] for p in stage), sample_basis, sample_table, grid)),
        )
        if begin:
            grid, vnew = out[:2]
        for p, back in zip(stage, out[2 * begin :]):
            returned[p] = exchange(back, p)
    velocity_new = vnew.reshape(gx, nyb, 3, layers, TILE).transpose(0, 1, 3, 2, 4)

    coef = pl.pallas_call(
        lambda *refs: unpack_kernel(sz, *refs),
        out_shape=shape((3, terms, cells), bf16),
        in_specs=vmem(1 + chunks),
        out_specs=vmem(1)[0],
        compiler_params=params,
        name="unpack",
    )(slot, *returned)
    return velocity_new, coef.transpose(2, 0, 1)


def solution(mesh):
    in_specs = (
        P("slab", "batch", None, None, None),
        P(("slab", "batch"), None, None),
        P(("slab", "batch"), None, None),
        P(("slab", "batch"), None),
        P(("slab", "batch"), None),
        P(("slab", "batch"), None),
        P(("slab", "batch")),
        P(),
        P(),
    )
    out_specs = (P("slab", "batch", None, None, None), P(("slab", "batch"), None, None))
    return jax.shard_map(local, mesh=mesh, in_specs=in_specs, out_specs=out_specs, check_vma=False)
```

```python
import math

import jax
import jax.numpy as jnp
from jax import lax
from jax.experimental import pallas as pl
from jax.experimental.pallas import tpu as pltpu
from jax.sharding import PartitionSpec as P

SWEEPS = 2
TILE = 128
GROUP = 8
MXU_LANES = 256
UNROLL = 12
DEAD = 64.0
MIDDLE = 64.0

kernel_width = 0.8
kernel_norm = 1.0 / (0.8 * math.sqrt(2.0 * math.pi))
coupling = 2.0
square = 0.5 / (math.log(2.0) * kernel_width * kernel_width)
norm_bits = math.log2(kernel_norm)

f32 = jnp.float32
bf16 = jnp.bfloat16


def round_up(value, step):
    return -(-value // step) * step


def iota(shape, dim):
    return lax.broadcasted_iota(jnp.int32, shape, dim)


def one_hot(mask):
    return jnp.where(mask, 1.0, 0.0).astype(bf16)


def dot(a, b, ca=1, cb=0):
    return lax.dot_general(a, b, (((ca,), (cb,)), ((), ())), preferred_element_type=f32)


def vmem(count=1):
    return [pl.BlockSpec(memory_space=pltpu.VMEM)] * count


params = pltpu.CompilerParams(vmem_limit_bytes=12 * 1024 * 1024)


class Sizes:
    def __init__(self, terms, points, stencil):
        self.terms, self.points, self.stencil = terms, points, stencil
        self.qw = round_up(points, TILE)
        self.cw = round_up(3 * terms, TILE)
        self.width = 3 * self.qw + self.cw
        self.mt = points // TILE * TILE
        self.mo = points - self.mt
        self.meta = 2 * stencil + 3
        self.rows = round_up(self.meta, 8)


def place_terms(sz, k):
    shape = (sz.cw, sz.terms)
    return one_hot(iota(shape, 0) == iota(shape, 1) + k * sz.terms)


def pieces(value, count):
    out = []
    for _ in range(count):
        part = value.astype(bf16).astype(f32)
        out.append(part)
        value = value - part
    return out


def pack_kernel(sz, slabs, cap, chunks, pairwise, ny, layers, *refs):
    owner, anchor, blocks, count, trac, offs = refs[:6]
    send, slot_out, rec = refs[6 : 6 + chunks], refs[6 + chunks], refs[7 + chunks]
    cells = owner.shape[1]
    slots = slabs * cap
    own = owner[...]
    member = one_hot(own == iota((slabs, cells), 0))
    before = one_hot(iota((cells, cells), 0) < iota((cells, cells), 1))
    rank = jnp.sum(member.astype(f32) * dot(member, before), axis=0, keepdims=True)
    if pairwise:
        slot = (own ^ lax.axis_index("slab")) * cap + rank.astype(jnp.int32)
    else:
        part = cap // chunks
        chunk = jnp.floor((rank + 0.5) * (1.0 / part))
        slot = (chunk * (slabs * part - part) + rank).astype(jnp.int32) + own * part
    slot_out[...] = slot
    place = one_hot(slot == iota((slots, cells), 0))

    tile = blocks[...].astype(f32)
    anchors = anchor[...].astype(f32)
    tile_x = jnp.floor((tile + 0.5) * (1.0 / (ny * layers)))
    tile_y = jnp.floor((tile + 0.5) * (1.0 / layers)) - tile_x * ny
    live = iota(tile.shape, 0) < count[...]
    dx = jnp.where(live, tile_x - anchors[0:1], DEAD)
    dy = jnp.where(live, tile_y - anchors[1:2], DEAD)

    rec[...] = jnp.zeros(rec.shape, bf16)
    for k in range(3):
        rec[:, k * sz.qw : k * sz.qw + sz.points] = offs[k]
    base = sz.mo
    meta = jnp.zeros((cells, TILE), f32)
    for row in (dx, dy, anchors):
        shape = (row.shape[0], TILE)
        where = one_hot(iota(shape, 1) == iota(shape, 0) + base)
        meta = meta + dot(row.astype(bf16), where, 0, 0)
        base += row.shape[0]
    rec[:, sz.mt : sz.mt + TILE] = rec[:, sz.mt : sz.mt + TILE] + meta.astype(bf16)
    coef = jnp.zeros((cells, sz.cw), f32)
    for k in range(3):
        coef = coef + dot(trac[k], place_terms(sz, k), 0, 1)
    rec[:, 3 * sz.qw :] = coef.astype(bf16)
    size = slots // chunks
    for c in range(chunks):
        send[c][...] = dot(place[c * size : (c + 1) * size], rec[...]).astype(bf16)


def load_records(sz, recv, points, lines):
    stencil = sz.stencil
    base = 0
    shape = (TILE, TILE)
    for part in recv:
        slots = part.shape[0]
        points[base : base + slots] = part[:, : 3 * sz.qw].astype(f32)
        meta = part[:, sz.mt : sz.mt + TILE]
        az = dot(meta, one_hot(iota(shape, 0) == sz.mo + 2 * stencil + 2))
        height = az - TILE * jnp.floor((az + 0.5) * (1.0 / TILE)) - MIDDLE
        for t in range(2 * sz.qw, 3 * sz.qw, TILE):
            points[base : base + slots, t : t + TILE] = points[base : base + slots, t : t + TILE] + height
        groups = slots // GROUP
        merge = one_hot(iota((groups, slots), 0) == iota((groups, slots), 1) // GROUP)
        mine = iota((slots, TILE), 0) % GROUP == iota((slots, TILE), 1) // stencil
        for d in range(2):
            spread = one_hot(iota(shape, 0) == iota(shape, 1) % stencil + sz.mo + d * stencil)
            lines[d, base // GROUP : base // GROUP + groups] = dot(
                merge, jnp.where(mine, dot(meta, spread), 0.0).astype(bf16)
            )
        base += slots


def height_table(shape, dim):
    cell, height = iota(shape, dim) // TILE, iota(shape, dim) % TILE
    kind, mine = iota(shape, 1 - dim) // GROUP, iota(shape, 1 - dim) % GROUP == cell
    m = height.astype(f32) - MIDDLE
    minus = pieces(-square * m * m, 3)
    value = jnp.where(kind < 3, m, jnp.where(kind < 6, 1.0, 0.0))
    for i in range(3):
        value = jnp.where(kind == 6 + i, minus[i], value)
    return jnp.where(mine, value, 0.0).astype(bf16)


def stack_rows(rows, like):
    rows = rows + [jnp.zeros_like(like)] * (TILE // GROUP - len(rows))
    return jnp.concatenate(rows, axis=0).astype(bf16)


def line_weights(sz, g, points, lines, w_ref):
    first = pl.multiple_of(g * GROUP, GROUP)
    pts = points[pl.ds(first, GROUP), : 2 * sz.qw]
    ox, oy = pts[:, : sz.qw], pts[:, sz.qw :]
    steps = [lines[d, pl.ds(g, 1), :] for d in range(2)]
    mine = iota((GROUP, TILE), 0) == iota((GROUP, TILE), 1) // sz.stencil
    dx, dy, norm = (jnp.where(mine, value, 0.0) for value in (*steps, steps[0] * steps[0] + steps[1] * steps[1]))
    unit = jnp.where(mine, 1.0, 0.0)
    left = stack_rows([dx, dx, dy, dy, unit, unit, norm, norm], dx)
    rows = pieces(2.0 * square * ox, 2) + pieces(2.0 * square * oy, 2)
    rows = rows + pieces(2.0 * norm_bits - square * (ox * ox + oy * oy), 2)
    rows = rows + pieces(jnp.full_like(ox, -square), 2)
    w_ref[...] = jnp.exp2(dot(left, stack_rows(rows, ox), 0, 0))


def height_factors(oz):
    rows = pieces(2.0 * square * oz, 3) + pieces(norm_bits - square * oz * oz, 3) + [jnp.ones_like(oz)] * 3
    return stack_rows(rows, oz)


def basis_kernel(sz, dim, basis, out, table):
    out[...] = jnp.zeros(out.shape, bf16)
    for k in range(3):
        points = slice(k * sz.qw, k * sz.qw + sz.points)
        if dim:
            out[:, points] = dot(place_terms(sz, k), basis[...]).astype(bf16)
        else:
            out[points] = dot(basis[...], place_terms(sz, k), 0, 1).astype(bf16)
    table[...] = height_table(table.shape, dim)


def in_turn(*works):
    works = list(works)
    while works:
        works = [work for work in works if next(work, works) is not works]


def run_groups(count, prepare, use, slots):
    in_turn(prepare(0, *slots[0]))
    turns = next(t for t in (UNROLL, 6, 4, 2, 1) if count % t == 0)

    def step(h, carry):
        for i in range(turns):
            g = turns * h + i
            if turns % 2:
                in_turn(use(g, *slots[0]))
                in_turn(prepare(g + 1, *slots[0]))
            else:
                in_turn(prepare(g + 1, *slots[(i + 1) % 2]), use(g, *slots[i % 2]))
        return carry

    lax.fori_loop(0, count // turns, step, 0)


def stencil_rows(sz, gx, ny, layers, meta):
    stencil, planes = sz.stencil, 3 * layers
    shape = (TILE, TILE)
    source, lane = iota(shape, 0) - sz.mo, iota(shape, 1)
    dx, dy = (dot(meta, one_hot((source == lane + d * stencil) & (lane < stencil))) for d in range(2))
    ax, ay, az = (dot(meta, one_hot(source == 2 * stencil + d)) for d in range(3))
    layer = jnp.floor((az + 0.5) * (1.0 / TILE))
    line = ((ax + dx) * ny + ay + dy) * planes + layer
    line = jnp.where((dx < 0.5 * DEAD) & (ax > 0.5), line, float(gx * planes * ny))
    return line


def spread_kernel(sz, gx, ny, nyb, layers, parts, begin, end, *refs):
    recv, (expand, table, start), refs = refs[:parts], refs[parts : 3 + parts], refs[3 + parts :]
    grid, rows_out = refs[0], refs[1 : 1 + parts]
    if end:
        keep, send = refs[1 + parts : 3 + parts]
    points, lines, forces, w0, wz0, w1, wz1, terms, rows_s, sem = refs[(3 if end else 1) + parts :]
    slots = points.shape[0]
    planes = 3 * layers
    stencil = sz.stencil
    count = slots // GROUP

    copies = []
    for i, part in enumerate(recv):
        size = part.shape[0]
        meta = part[:, sz.mt : sz.mt + TILE]
        rows_out[i][...] = stencil_rows(sz, gx, ny, layers, meta).astype(jnp.int32)
        copies.append(pltpu.make_async_copy(rows_out[i], rows_s.at[pl.ds(i * size, size)], sem.at[i]))
        copies[-1].start()
    load_records(sz, recv, points, lines)
    forces[...] = dot(jnp.concatenate([part[:, 3 * sz.qw :] for part in recv], axis=0), expand[...])
    if begin:
        grid[...] = jnp.zeros(grid.shape, f32)
        size = nyb * planes
        for x in range(gx):
            grid[pl.ds(pl.multiple_of(x * ny * planes + lax.axis_index("batch") * size, 8), size), :] = start[x * size : (x + 1) * size]
    for copy in copies:
        copy.wait()

    def prepare(g, w_ref, wz_ref):
        g = jnp.minimum(g, count - 1)
        line_weights(sz, g, points, lines, w_ref)
        oz = points[pl.ds(pl.multiple_of(g * GROUP, GROUP), GROUP), 2 * sz.qw :]
        left = jnp.transpose(height_factors(oz))
        yield
        for u in range(0, GROUP * TILE, 2 * TILE):
            for t in range(0, sz.qw, TILE):
                exponents = dot(left[t : t + TILE], table[:, u : u + 2 * TILE])
                wz_ref[t : t + TILE, u : u + 2 * TILE] = jnp.exp2(exponents).astype(bf16)
                yield

    def use(g, w_ref, wz_ref):
        first = pl.multiple_of(g * GROUP, GROUP)
        frc = forces[pl.ds(first, GROUP), :]
        for u in range(GROUP):
            w = w_ref[u * stencil : (u + 1) * stencil]
            weighted = [(frc[u : u + 1, k * sz.qw : (k + 1) * sz.qw] * w).astype(bf16) for k in range(3)]
            sums = dot(jnp.concatenate(weighted, axis=0), wz_ref[:, u * TILE : (u + 1) * TILE])
            for k in range(3):
                for j in range(0, stencil, 8):
                    terms[u, pl.ds(4 * j + k, 8, stride=4), :] = sums[k * stencil + j : k * stencil + j + 8]
            yield
            spots = [pl.ds(rows_s[first + u, j], 3, stride=layers) for j in range(stencil)]
            sums = [grid[spots[j], :] + terms[u, 4 * j : 4 * j + 3] for j in range(stencil)]
            for j in range(stencil):
                grid[spots[j], :] = sums[j]

    run_groups(count, prepare, use, ((w0, wz0), (w1, wz1)))

    if end:
        half = ny // 2 * planes
        mine = lax.axis_index("batch") % 2
        for x in range(gx):
            for ref, part in ((keep, mine), (send, 1 - mine)):
                rows = grid[pl.ds(pl.multiple_of((2 * x + part) * half, 8), half), :]
                ref[x * half : (x + 1) * half] = rows.astype(bf16)


def relax(gx, ny, layers, slabs, own, other, drive, state, last):
    planes = 3 * layers
    rows = ny * planes
    half = rows // 2
    pad = (drive.shape[1] - rows) // 2
    wide = gx + 2 * SWEEPS
    edge = jnp.zeros((pad, TILE), f32)
    mine = lax.axis_index("batch") % 2

    def load(p, carry):
        for ref, part in ((own, mine), (other, 1 - mine)):
            values = ref[pl.ds(pl.multiple_of(p * half, 16), half), :].astype(f32)
            drive[p, pl.ds(pl.multiple_of(pad + part * half, 8), half), :] = values
        for ref in (drive, state):
            ref[p, 0:pad] = edge
            ref[p, pad + rows :] = edge
        return carry

    lax.fori_loop(0, wide, load, 0)

    size = 8 * planes
    lane = iota((size, TILE), 1)
    layer = iota((size, TILE), 0) % layers
    last_lane, first_lane = lane == TILE - 1, lane == 0
    above = jnp.where(layer < layers - 1, 1.0, 0.0)
    below = jnp.where(layer > 0, 1.0, 0.0)

    def sweep(source, p, store):
        for at in range(0, rows, size):
            def near(step):
                return source[p, pl.ds(pad + at + step, size), :]

            upper = pltpu.roll(jnp.where(first_lane, near(1) * above, near(0)), TILE - 1, 1)
            lower = pltpu.roll(jnp.where(last_lane, near(-1) * below, near(0)), 1, 1)
            around = source[p - 1, pl.ds(pad + at, size), :] + source[p + 1, pl.ds(pad + at, size), :]
            around = around + near(planes) + near(-planes) + upper + lower
            centre = drive[p, pl.ds(pad + at, size), :]
            store(p, at, (centre + coupling * around) * (1.0 / (1.0 + 6.0 * coupling)))

    def first_sweep(p, carry):
        inside = ((p >= SWEEPS) | (lax.axis_index("slab") > 0)) & ((p < gx + SWEEPS) | (lax.axis_index("slab") < slabs - 1))
        factor = inside.astype(f32)

        def store(p, at, value):
            state[p, pl.ds(pad + at, size), :] = value * factor

        sweep(drive, p, store)
        return carry

    lax.fori_loop(1, wide - 1, first_sweep, 0)

    def second_sweep(p, carry):
        def store(p, at, value):
            last[pl.ds(pl.multiple_of((p - SWEEPS) * rows + at, 8), size), :] = value

        sweep(state, p, store)
        return carry

    lax.fori_loop(SWEEPS, gx + SWEEPS, second_sweep, 0)
    last[gx * rows :] = jnp.zeros((last.shape[0] - gx * rows, TILE), f32)


def sample_weights(sz, g, points, lines, table, w_ref, wz_ref):
    cut = sz.qw // MXU_LANES * MXU_LANES
    heights = (iota((TILE, TILE), 0).astype(f32) - MIDDLE) * math.sqrt(square)
    line_weights(sz, g, points, lines, w_ref)
    oz = points[pl.ds(pl.multiple_of(g * GROUP, GROUP), GROUP), 2 * sz.qw :]
    right = height_factors(oz[:, :cut]) if cut else None
    rest = oz[:, cut:] * math.sqrt(square)
    yield
    for u in range(GROUP):
        if cut:
            exponents = dot(table[u * TILE : (u + 1) * TILE], right)
            wz_ref[u * TILE : (u + 1) * TILE, :cut] = jnp.exp2(exponents).astype(bf16)
        for t in range(cut, sz.qw, TILE):
            away = rest[u : u + 1, t - cut : t - cut + TILE] - heights
            value = jnp.exp2(norm_bits - away * away).astype(bf16)
            wz_ref[u * TILE : (u + 1) * TILE, t : t + TILE] = value
        yield


def weights_kernel(sz, parts, *refs):
    recv, (table, w_out, wz_out, points, lines) = refs[:parts], refs[parts:]
    load_records(sz, recv, points, lines)
    count = w_out.shape[0]
    turns = next(t for t in (4, 2, 1) if count % t == 0)

    def step(h, carry):
        groups = [turns * h + i for i in range(turns)]
        for g in groups:
            in_turn(sample_weights(sz, g, points, lines, table, w_out.at[g], wz_out.at[g]))
        return carry

    lax.fori_loop(0, count // turns, step, 0)


def sample_kernel(sz, gx, ny, nyb, layers, slabs, parts, begin, halves, *refs):
    lines_in, refs = refs[:parts], refs[parts:]
    if begin:
        ready, refs = refs[: 2 * halves], refs[2 * halves :]
        expand, own, other, last, vnew = refs[:5]
        back, (drive, state, *refs) = refs[5 : 5 + parts], refs[5 + parts :]
    else:
        recv, (expand, table, last), refs = refs[:parts], refs[parts : 3 + parts], refs[3 + parts :]
        back, (points, lines, w0, wz0, w1, wz1, *refs) = refs[:parts], refs[parts:]
    gathered, products, sampled, rows_s, sem = refs
    copies = []
    for i, part in enumerate(lines_in):
        size = part.shape[0]
        copies.append(pltpu.make_async_copy(part, rows_s.at[pl.ds(i * size, size)], sem.at[i]))
        copies[-1].start()
    stencil = sz.stencil
    slots = sampled.shape[0]
    count = slots // GROUP
    planes = 3 * layers
    if not begin:
        load_records(sz, recv, points, lines)
    else:
        relax(gx, ny, layers, slabs, own, other, drive, state, last)
        size = nyb * planes
        for x in range(gx):
            at = pl.multiple_of(x * ny * planes + lax.axis_index("batch") * size, 8)
            vnew[x * size : (x + 1) * size] = last[pl.ds(at, size), :]
    shape = (3 * GROUP, 3 * GROUP * stencil)
    cell, part = iota(shape, 1) // (3 * stencil), iota(shape, 1) // stencil % 3
    adds = one_hot(iota(shape, 0) == part * GROUP + cell)

    for copy in copies:
        copy.wait()
    def prepare(g, w_ref, wz_ref):
        yield from sample_weights(sz, jnp.minimum(g, count - 1), points, lines, table, w_ref, wz_ref)

    def use(g, w_ref, wz_ref):
        first = pl.multiple_of(g * GROUP, GROUP)
        for u in range(GROUP):
            for j in range(stencil):
                spot = pl.ds(rows_s[first + u, j], 3, stride=layers)
                gathered[u, 4 * j : 4 * j + 3] = last[spot, :]
        for u in range(GROUP):
            tiles = [
                gathered[u, pl.ds(4 * j + k, 8, stride=4), :] for k in range(3) for j in range(0, stencil, 8)
            ]
            projected = dot(jnp.concatenate(tiles, axis=0).astype(bf16), wz_ref[u * TILE : (u + 1) * TILE])
            w = w_ref[u * stencil : (u + 1) * stencil]
            for k in range(3):
                at = (u * 3 + k) * stencil
                products[at : at + stencil] = (projected[k * stencil : (k + 1) * stencil] * w).astype(bf16)
            yield
        values = dot(adds, products[...])
        for k in range(3):
            sampled[pl.ds(first, GROUP), k * sz.qw : (k + 1) * sz.qw] = values[k * GROUP : (k + 1) * GROUP]

    def use_ready(base, w_in, wz_in):
        turns = next(t for t in (UNROLL, 6, 4, 2, 1) if w_in.shape[0] % t == 0)

        def step(h, carry):
            for i in range(turns):
                g = turns * h + i
                in_turn(use(base + g, w_in.at[g], wz_in.at[g]))
            return carry

        lax.fori_loop(0, w_in.shape[0] // turns, step, 0)

    if begin:
        base = 0
        for w_in, wz_in in zip(ready[::2], ready[1::2]):
            use_ready(base, w_in, wz_in)
            base += w_in.shape[0]
    else:
        run_groups(count, prepare, use, ((w0, wz0), (w1, wz1)))
    coef = dot(sampled[...].astype(bf16), expand[...]).astype(bf16)
    base = 0
    for ref in back:
        ref[...] = coef[base : base + ref.shape[0]]
        base += ref.shape[0]


def unpack_kernel(sz, *refs):
    slot, out = refs[0], refs[-1]
    parts = refs[1:-1]
    cells, size = slot.shape[1], parts[0].shape[0]
    coef = jnp.zeros((cells, sz.cw), f32)
    for c, back in enumerate(parts):
        place = one_hot(slot[...] == iota((size, cells), 0) + c * size)
        coef = coef + dot(place, back[...], 0, 0)
    coef = coef.astype(bf16)
    for k in range(3):
        shape = (sz.terms, sz.cw)
        pick = one_hot(iota(shape, 1) == iota(shape, 0) + k * sz.terms)
        out[k] = dot(pick, coef, 1, 1).astype(bf16)


def local(
    velocity_old, traction, offsets, owner_slab, anchor, blocks, block_count, synthesis, analysis
):
    cells, _, terms = traction.shape
    gx, nyb, layers = velocity_old.shape[:3]
    slabs, batches = lax.axis_size("slab"), lax.axis_size("batch")
    ny = nyb * batches
    planes = 3 * layers
    cap = 2 * cells // slabs
    stencil = blocks.shape[1]
    sz = Sizes(terms, offsets.shape[2], stencil)
    half = ny // 2
    grid_rows = gx * ny * planes + 8 * planes

    pairwise = cap % 16 == 0 and slabs & (slabs - 1) == 0
    if pairwise:
        chunks, size = slabs, cap
        stages = [list(range(min(4, slabs)))] + ([list(range(4, slabs))] if slabs > 4 else [])
        back_stages = [list(range(4, slabs)), list(range(1, min(4, slabs))), [0]]
        back_stages = [stage for stage in back_stages if stage]
    else:
        chunks = next(c for c in (3, 2, 1) if cap % c == 0 and slabs * (cap // c) % 16 == 0)
        size = slabs * cap // chunks
        stages = back_stages = [[c] for c in range(chunks)]

    def exchange(value, p):
        if not pairwise:
            return lax.all_to_all(value, "slab", split_axis=0, concat_axis=0, tiled=True)
        return lax.ppermute(value, "slab", [(i, i ^ p) for i in range(slabs)]) if p else value

    def shape(dims, dtype):
        return jax.ShapeDtypeStruct(dims, dtype)

    def whole(dims):
        return pl.BlockSpec(dims, lambda i: (0,) * len(dims))

    packed = [
        owner_slab.T,
        anchor.T,
        blocks.T,
        block_count.reshape(1, cells),
        traction.transpose(1, 2, 0),
        offsets.transpose(1, 0, 2),
    ]
    send = pl.pallas_call(
        lambda *refs: pack_kernel(sz, slabs, cap, chunks, pairwise, ny, layers, *refs),
        grid=(1,),
        out_shape=[shape((size, sz.width), bf16)] * chunks + [shape((1, cells), jnp.int32)],
        in_specs=[whole(value.shape) for value in packed],
        out_specs=[whole((size, sz.width))] * chunks + [whole((1, cells))],
        scratch_shapes=[pltpu.VMEM((cells, sz.width), bf16)],
        compiler_params=pltpu.CompilerParams(vmem_limit_bytes=60 * 1024 * 1024),
        name="pack",
    )(*packed)
    slot = send[chunks]
    recv = [exchange(send[p], p) for p in range(chunks)]

    def basis(values, dim):
        table = (TILE, GROUP * TILE) if dim else (GROUP * TILE, TILE)
        return pl.pallas_call(
            lambda *refs: basis_kernel(sz, dim, *refs),
            out_shape=[shape((sz.cw, 3 * sz.qw) if dim else (3 * sz.qw, sz.cw), bf16), shape(table, bf16)],
            in_specs=vmem(1),
            out_specs=vmem(2),
            compiler_params=params,
            name="basis",
        )(values)

    spread_basis, spread_table = basis(synthesis, 1)

    grid_shape = shape((grid_rows, TILE), f32)
    half_shape = shape((gx * planes * half, TILE), bf16)
    weights_xy = pltpu.VMEM((GROUP * stencil, sz.qw), f32)
    terms_shape = pltpu.VMEM((GROUP, 4 * stencil, TILE), f32)
    grid = velocity_old.transpose(0, 1, 3, 2, 4).reshape(-1, TILE)
    rows = {}
    for stage in stages:
        parts = len(stage)
        slots = parts * size
        begin, end = stage is stages[0], stage is stages[-1]
        points = [pltpu.VMEM((slots, 3 * sz.qw), f32), pltpu.VMEM((2, slots // GROUP, TILE), f32)]
        out = pl.pallas_call(
            lambda *refs: spread_kernel(sz, gx, ny, nyb, layers, parts, begin, end, *refs),
            out_shape=[
                grid_shape,
            ]
            + [shape((size, TILE), jnp.int32)] * parts
            + [half_shape] * (2 * end),
            in_specs=vmem(parts + 3),
            out_specs=vmem(1 + parts + 2 * end),
            scratch_shapes=points
            + [pltpu.VMEM((slots, 3 * sz.qw), f32)]
            + [weights_xy, pltpu.VMEM((sz.qw, GROUP * TILE), bf16)] * 2
            + [terms_shape, pltpu.SMEM((slots, TILE), jnp.int32), pltpu.SemaphoreType.DMA((parts,))],
            input_output_aliases={} if begin else {2 + parts: 0},
            compiler_params=params,
            cost_estimate=pl.CostEstimate(flops=100_000_000 * slots, bytes_accessed=4_000_000, transcendentals=0),
            name="spread",
        )(*(recv[p] for p in stage), spread_basis, spread_table, grid)
        grid = out[0]
        rows.update(zip(stage, out[1 : 1 + parts]))
    keep, send_half = out[-2:]

    def pairs(bit):
        return [(i, i ^ bit) for i in range(batches)]

    def add(a, b):
        return (a.astype(f32) + b.astype(f32)).astype(bf16)

    mine = add(keep, lax.ppermute(send_half, "batch", pairs(1)))
    def weights(values):
        slots = len(values) * size
        groups = slots // GROUP
        return pl.pallas_call(
            lambda *refs: weights_kernel(sz, len(values), *refs),
            out_shape=[
                shape((groups, GROUP * stencil, sz.qw), f32),
                shape((groups, GROUP * TILE, sz.qw), bf16),
            ],
            in_specs=vmem(len(values) + 1),
            out_specs=vmem(2),
            scratch_shapes=[pltpu.VMEM((slots, 3 * sz.qw), f32), pltpu.VMEM((2, groups, TILE), f32)],
            compiler_params=params,
            cost_estimate=pl.CostEstimate(flops=50_000_000 * slots, bytes_accessed=4_000_000, transcendentals=0),
            name="weights",
        )(*values, sample_table)

    first = back_stages[0]
    late = [recv[p] for p in first]
    mine, analysis, late = lax.optimization_barrier((mine, analysis, late))
    sample_basis, sample_table = basis(analysis, 0)
    ready = [weights(late[: (len(late) + 1) // 2])]
    halo = SWEEPS * planes * half
    low = lax.ppermute(mine[-halo:], "slab", [(i, i + 1) for i in range(slabs - 1)])
    high = lax.ppermute(mine[:halo], "slab", [(i + 1, i) for i in range(slabs - 1)])
    edges = jnp.concatenate([low, high], axis=0)
    bit = 2
    while bit < batches:
        got = lax.ppermute(mine, "batch", pairs(bit))
        edges, got, ready, late = lax.optimization_barrier((edges, got, ready, late))
        mine = add(mine, got)
        edges = add(edges, lax.ppermute(edges, "batch", pairs(bit)))
        bit *= 2
    mine = jnp.concatenate([edges[:halo], mine, edges[halo:]], axis=0)
    if len(late) > 1:
        ready.append(weights(late[(len(late) + 1) // 2 :]))
        mine, ready = lax.optimization_barrier((mine, ready))
    other = lax.ppermute(mine, "batch", pairs(1))

    wide = gx + 2 * SWEEPS
    padded = pltpu.VMEM((wide, planes * ny + 16, TILE), f32)
    returned = [None] * chunks
    for stage in back_stages:
        parts = len(stage)
        slots = parts * size
        begin = stage is back_stages[0]
        out = pl.pallas_call(
            lambda *refs: sample_kernel(sz, gx, ny, nyb, layers, slabs, parts, begin, len(ready), *refs),
            out_shape=([grid_shape, shape((gx * nyb * planes, TILE), f32)] if begin else [])
            + [shape((size, sz.cw), bf16)] * parts,
            in_specs=vmem(parts + 2 * len(ready) + 3 if begin else 2 * parts + 3),
            out_specs=vmem(2 * begin + parts),
            scratch_shapes=(
                [padded, padded]
                if begin
                else [pltpu.VMEM((slots, 3 * sz.qw), f32), pltpu.VMEM((2, slots // GROUP, TILE), f32)]
                + [weights_xy, pltpu.VMEM((GROUP * TILE, sz.qw), bf16)] * 2
            )
            + [terms_shape]
            + [pltpu.VMEM((3 * GROUP * stencil, sz.qw), bf16), pltpu.VMEM((slots, 3 * sz.qw), f32)]
            + [pltpu.SMEM((slots, TILE), jnp.int32), pltpu.SemaphoreType.DMA((parts,))],
            compiler_params=params,
            cost_estimate=pl.CostEstimate(flops=50_000_000 * slots, bytes_accessed=4_000_000, transcendentals=0),
            name="sample",
        )(
            *(rows[p] for p in stage),
            *((*sum(map(list, ready), []), sample_basis, mine, other) if begin else (*(recv[p] for p in stage), sample_basis, sample_table, grid)),
        )
        if begin:
            grid, vnew = out[:2]
        for p, back in zip(stage, out[2 * begin :]):
            returned[p] = exchange(back, p)
    velocity_new = vnew.reshape(gx, nyb, 3, layers, TILE).transpose(0, 1, 3, 2, 4)

    coef = pl.pallas_call(
        lambda *refs: unpack_kernel(sz, *refs),
        out_shape=shape((3, terms, cells), bf16),
        in_specs=vmem(1 + chunks),
        out_specs=vmem(1)[0],
        compiler_params=params,
        name="unpack",
    )(slot, *returned)
    return velocity_new, coef.transpose(2, 0, 1)


def solution(mesh):
    in_specs = (
        P("slab", "batch", None, None, None),
        P(("slab", "batch"), None, None),
        P(("slab", "batch"), None, None),
        P(("slab", "batch"), None),
        P(("slab", "batch"), None),
        P(("slab", "batch"), None),
        P(("slab", "batch")),
        P(),
        P(),
    )
    out_specs = (P("slab", "batch", None, None, None), P(("slab", "batch"), None, None))
    return jax.shard_map(local, mesh=mesh, in_specs=in_specs, out_specs=out_specs, check_vma=False)
```

```python
import math

import jax
import jax.numpy as jnp
from jax import lax
from jax.experimental import pallas as pl
from jax.experimental.pallas import tpu as pltpu
from jax.sharding import PartitionSpec as P

SWEEPS = 2
TILE = 128
GROUP = 8
MXU_LANES = 256
UNROLL = 12
DEAD = 64.0
MIDDLE = 64.0

kernel_width = 0.8
kernel_norm = 1.0 / (0.8 * math.sqrt(2.0 * math.pi))
coupling = 2.0
square = 0.5 / (math.log(2.0) * kernel_width * kernel_width)
norm_bits = math.log2(kernel_norm)

f32 = jnp.float32
bf16 = jnp.bfloat16


def round_up(value, step):
    return -(-value // step) * step


def iota(shape, dim):
    return lax.broadcasted_iota(jnp.int32, shape, dim)


def one_hot(mask):
    return jnp.where(mask, 1.0, 0.0).astype(bf16)


def dot(a, b, ca=1, cb=0):
    return lax.dot_general(a, b, (((ca,), (cb,)), ((), ())), preferred_element_type=f32)


def vmem(count=1):
    return [pl.BlockSpec(memory_space=pltpu.VMEM)] * count


params = pltpu.CompilerParams(vmem_limit_bytes=12 * 1024 * 1024)


class Sizes:
    def __init__(self, terms, points, stencil):
        self.terms, self.points, self.stencil = terms, points, stencil
        self.qw = round_up(points, TILE)
        self.cw = round_up(3 * terms, TILE)
        self.width = 3 * self.qw + self.cw
        self.mt = points // TILE * TILE
        self.mo = points - self.mt
        self.meta = 2 * stencil + 3
        self.rows = round_up(self.meta, 8)


def place_terms(sz, k):
    shape = (sz.cw, sz.terms)
    return one_hot(iota(shape, 0) == iota(shape, 1) + k * sz.terms)


def pieces(value, count):
    out = []
    for _ in range(count):
        part = value.astype(bf16).astype(f32)
        out.append(part)
        value = value - part
    return out


def pack_kernel(sz, slabs, cap, chunks, pairwise, ny, layers, *refs):
    owner, anchor, blocks, count, trac, offs = refs[:6]
    send, slot_out, rec = refs[6 : 6 + chunks], refs[6 + chunks], refs[7 + chunks]
    cells = owner.shape[1]
    slots = slabs * cap
    own = owner[...]
    member = one_hot(own == iota((slabs, cells), 0))
    before = one_hot(iota((cells, cells), 0) < iota((cells, cells), 1))
    rank = jnp.sum(member.astype(f32) * dot(member, before), axis=0, keepdims=True)
    if pairwise:
        slot = (own ^ lax.axis_index("slab")) * cap + rank.astype(jnp.int32)
    else:
        part = cap // chunks
        chunk = jnp.floor((rank + 0.5) * (1.0 / part))
        slot = (chunk * (slabs * part - part) + rank).astype(jnp.int32) + own * part
    slot_out[...] = slot
    place = one_hot(slot == iota((slots, cells), 0))

    tile = blocks[...].astype(f32)
    anchors = anchor[...].astype(f32)
    tile_x = jnp.floor((tile + 0.5) * (1.0 / (ny * layers)))
    tile_y = jnp.floor((tile + 0.5) * (1.0 / layers)) - tile_x * ny
    live = iota(tile.shape, 0) < count[...]
    dx = jnp.where(live, tile_x - anchors[0:1], DEAD)
    dy = jnp.where(live, tile_y - anchors[1:2], DEAD)

    rec[...] = jnp.zeros(rec.shape, bf16)
    for k in range(3):
        rec[:, k * sz.qw : k * sz.qw + sz.points] = offs[k]
    base = sz.mo
    meta = jnp.zeros((cells, TILE), f32)
    for row in (dx, dy, anchors):
        shape = (row.shape[0], TILE)
        where = one_hot(iota(shape, 1) == iota(shape, 0) + base)
        meta = meta + dot(row.astype(bf16), where, 0, 0)
        base += row.shape[0]
    rec[:, sz.mt : sz.mt + TILE] = rec[:, sz.mt : sz.mt + TILE] + meta.astype(bf16)
    coef = jnp.zeros((cells, sz.cw), f32)
    for k in range(3):
        coef = coef + dot(trac[k], place_terms(sz, k), 0, 1)
    rec[:, 3 * sz.qw :] = coef.astype(bf16)
    size = slots // chunks
    for c in range(chunks):
        send[c][...] = dot(place[c * size : (c + 1) * size], rec[...]).astype(bf16)


def load_records(sz, recv, points, lines):
    stencil = sz.stencil
    base = 0
    shape = (TILE, TILE)
    for part in recv:
        slots = part.shape[0]
        points[base : base + slots] = part[:, : 3 * sz.qw].astype(f32)
        meta = part[:, sz.mt : sz.mt + TILE]
        az = dot(meta, one_hot(iota(shape, 0) == sz.mo + 2 * stencil + 2))
        height = az - TILE * jnp.floor((az + 0.5) * (1.0 / TILE)) - MIDDLE
        for t in range(2 * sz.qw, 3 * sz.qw, TILE):
            points[base : base + slots, t : t + TILE] = points[base : base + slots, t : t + TILE] + height
        groups = slots // GROUP
        merge = one_hot(iota((groups, slots), 0) == iota((groups, slots), 1) // GROUP)
        mine = iota((slots, TILE), 0) % GROUP == iota((slots, TILE), 1) // stencil
        for d in range(2):
            spread = one_hot(iota(shape, 0) == iota(shape, 1) % stencil + sz.mo + d * stencil)
            lines[d, base // GROUP : base // GROUP + groups] = dot(
                merge, jnp.where(mine, dot(meta, spread), 0.0).astype(bf16)
            )
        base += slots


def height_table(shape, dim):
    cell, height = iota(shape, dim) // TILE, iota(shape, dim) % TILE
    kind, mine = iota(shape, 1 - dim) // GROUP, iota(shape, 1 - dim) % GROUP == cell
    m = height.astype(f32) - MIDDLE
    minus = pieces(-square * m * m, 3)
    value = jnp.where(kind < 3, m, jnp.where(kind < 6, 1.0, 0.0))
    for i in range(3):
        value = jnp.where(kind == 6 + i, minus[i], value)
    return jnp.where(mine, value, 0.0).astype(bf16)


def stack_rows(rows, like):
    rows = rows + [jnp.zeros_like(like)] * (TILE // GROUP - len(rows))
    return jnp.concatenate(rows, axis=0).astype(bf16)


def line_weights(sz, g, points, lines, w_ref):
    first = pl.multiple_of(g * GROUP, GROUP)
    pts = points[pl.ds(first, GROUP), : 2 * sz.qw]
    ox, oy = pts[:, : sz.qw], pts[:, sz.qw :]
    steps = [lines[d, pl.ds(g, 1), :] for d in range(2)]
    mine = iota((GROUP, TILE), 0) == iota((GROUP, TILE), 1) // sz.stencil
    dx, dy, norm = (jnp.where(mine, value, 0.0) for value in (*steps, steps[0] * steps[0] + steps[1] * steps[1]))
    unit = jnp.where(mine, 1.0, 0.0)
    left = stack_rows([dx, dx, dy, dy, unit, unit, norm, norm], dx)
    rows = pieces(2.0 * square * ox, 2) + pieces(2.0 * square * oy, 2)
    rows = rows + pieces(2.0 * norm_bits - square * (ox * ox + oy * oy), 2)
    rows = rows + pieces(jnp.full_like(ox, -square), 2)
    w_ref[...] = jnp.exp2(dot(left, stack_rows(rows, ox), 0, 0))


def height_factors(oz):
    rows = pieces(2.0 * square * oz, 3) + pieces(norm_bits - square * oz * oz, 3) + [jnp.ones_like(oz)] * 3
    return stack_rows(rows, oz)


def basis_kernel(sz, dim, basis, out, table):
    out[...] = jnp.zeros(out.shape, bf16)
    for k in range(3):
        points = slice(k * sz.qw, k * sz.qw + sz.points)
        if dim:
            out[:, points] = dot(place_terms(sz, k), basis[...]).astype(bf16)
        else:
            out[points] = dot(basis[...], place_terms(sz, k), 0, 1).astype(bf16)
    table[...] = height_table(table.shape, dim)


def in_turn(*works):
    works = list(works)
    while works:
        works = [work for work in works if next(work, works) is not works]


def run_groups(count, prepare, use, slots):
    in_turn(prepare(0, *slots[0]))
    turns = next(t for t in (UNROLL, 6, 4, 2, 1) if count % t == 0)

    def step(h, carry):
        for i in range(turns):
            g = turns * h + i
            if turns % 2:
                in_turn(use(g, *slots[0]))
                in_turn(prepare(g + 1, *slots[0]))
            else:
                in_turn(prepare(g + 1, *slots[(i + 1) % 2]), use(g, *slots[i % 2]))
        return carry

    lax.fori_loop(0, count // turns, step, 0)


def stencil_rows(sz, gx, ny, layers, meta):
    stencil, planes = sz.stencil, 3 * layers
    shape = (TILE, TILE)
    source, lane = iota(shape, 0) - sz.mo, iota(shape, 1)
    dx, dy = (dot(meta, one_hot((source == lane + d * stencil) & (lane < stencil))) for d in range(2))
    ax, ay, az = (dot(meta, one_hot(source == 2 * stencil + d)) for d in range(3))
    layer = jnp.floor((az + 0.5) * (1.0 / TILE))
    line = ((ax + dx) * ny + ay + dy) * planes + layer
    line = jnp.where((dx < 0.5 * DEAD) & (ax > 0.5), line, float(gx * planes * ny))
    return line


def spread_kernel(sz, gx, ny, nyb, layers, parts, begin, end, *refs):
    recv, (expand, table, start), refs = refs[:parts], refs[parts : 3 + parts], refs[3 + parts :]
    grid, rows_out = refs[0], refs[1 : 1 + parts]
    if end:
        keep, send = refs[1 + parts : 3 + parts]
    points, lines, forces, w0, wz0, w1, wz1, terms, rows_s, sem = refs[(3 if end else 1) + parts :]
    slots = points.shape[0]
    planes = 3 * layers
    stencil = sz.stencil
    count = slots // GROUP

    copies = []
    for i, part in enumerate(recv):
        size = part.shape[0]
        meta = part[:, sz.mt : sz.mt + TILE]
        rows_out[i][...] = stencil_rows(sz, gx, ny, layers, meta).astype(jnp.int32)
        copies.append(pltpu.make_async_copy(rows_out[i], rows_s.at[pl.ds(i * size, size)], sem.at[i]))
        copies[-1].start()
    load_records(sz, recv, points, lines)
    forces[...] = dot(jnp.concatenate([part[:, 3 * sz.qw :] for part in recv], axis=0), expand[...])
    if begin:
        grid[...] = jnp.zeros(grid.shape, f32)
        size = nyb * planes
        for x in range(gx):
            grid[pl.ds(pl.multiple_of(x * ny * planes + lax.axis_index("batch") * size, 8), size), :] = start[x * size : (x + 1) * size]
    for copy in copies:
        copy.wait()

    def prepare(g, w_ref, wz_ref):
        g = jnp.minimum(g, count - 1)
        line_weights(sz, g, points, lines, w_ref)
        oz = points[pl.ds(pl.multiple_of(g * GROUP, GROUP), GROUP), 2 * sz.qw :]
        left = jnp.transpose(height_factors(oz))
        yield
        for u in range(0, GROUP * TILE, 2 * TILE):
            for t in range(0, sz.qw, TILE):
                exponents = dot(left[t : t + TILE], table[:, u : u + 2 * TILE])
                wz_ref[t : t + TILE, u : u + 2 * TILE] = jnp.exp2(exponents).astype(bf16)
                yield

    def use(g, w_ref, wz_ref):
        first = pl.multiple_of(g * GROUP, GROUP)
        frc = forces[pl.ds(first, GROUP), :]
        for u in range(GROUP):
            w = w_ref[u * stencil : (u + 1) * stencil]
            weighted = [(frc[u : u + 1, k * sz.qw : (k + 1) * sz.qw] * w).astype(bf16) for k in range(3)]
            sums = dot(jnp.concatenate(weighted, axis=0), wz_ref[:, u * TILE : (u + 1) * TILE])
            for k in range(3):
                for j in range(0, stencil, 8):
                    terms[u, pl.ds(4 * j + k, 8, stride=4), :] = sums[k * stencil + j : k * stencil + j + 8]
            yield
            spots = [pl.ds(rows_s[first + u, j], 3, stride=layers) for j in range(stencil)]
            sums = [grid[spots[j], :] + terms[u, 4 * j : 4 * j + 3] for j in range(stencil)]
            for j in range(stencil):
                grid[spots[j], :] = sums[j]

    run_groups(count, prepare, use, ((w0, wz0), (w1, wz1)))

    if end:
        half = ny // 2 * planes
        mine = lax.axis_index("batch") % 2
        for x in range(gx):
            for ref, part in ((keep, mine), (send, 1 - mine)):
                rows = grid[pl.ds(pl.multiple_of((2 * x + part) * half, 8), half), :]
                ref[x * half : (x + 1) * half] = rows.astype(bf16)


def relax(gx, ny, layers, slabs, own, other, drive, state, last):
    planes = 3 * layers
    rows = ny * planes
    half = rows // 2
    pad = (drive.shape[1] - rows) // 2
    wide = gx + 2 * SWEEPS
    edge = jnp.zeros((pad, TILE), f32)
    mine = lax.axis_index("batch") % 2

    def load(p, carry):
        for ref, part in ((own, mine), (other, 1 - mine)):
            values = ref[pl.ds(pl.multiple_of(p * half, 16), half), :].astype(f32)
            drive[p, pl.ds(pl.multiple_of(pad + part * half, 8), half), :] = values
        for ref in (drive, state):
            ref[p, 0:pad] = edge
            ref[p, pad + rows :] = edge
        return carry

    lax.fori_loop(0, wide, load, 0)

    size = 8 * planes
    lane = iota((size, TILE), 1)
    layer = iota((size, TILE), 0) % layers
    last_lane, first_lane = lane == TILE - 1, lane == 0
    above = jnp.where(layer < layers - 1, 1.0, 0.0)
    below = jnp.where(layer > 0, 1.0, 0.0)

    def sweep(source, p, store):
        for at in range(0, rows, size):
            def near(step):
                return source[p, pl.ds(pad + at + step, size), :]

            upper = pltpu.roll(jnp.where(first_lane, near(1) * above, near(0)), TILE - 1, 1)
            lower = pltpu.roll(jnp.where(last_lane, near(-1) * below, near(0)), 1, 1)
            around = source[p - 1, pl.ds(pad + at, size), :] + source[p + 1, pl.ds(pad + at, size), :]
            around = around + near(planes) + near(-planes) + upper + lower
            centre = drive[p, pl.ds(pad + at, size), :]
            store(p, at, (centre + coupling * around) * (1.0 / (1.0 + 6.0 * coupling)))

    def first_sweep(p, carry):
        inside = ((p >= SWEEPS) | (lax.axis_index("slab") > 0)) & ((p < gx + SWEEPS) | (lax.axis_index("slab") < slabs - 1))
        factor = inside.astype(f32)

        def store(p, at, value):
            state[p, pl.ds(pad + at, size), :] = value * factor

        sweep(drive, p, store)
        return carry

    lax.fori_loop(1, wide - 1, first_sweep, 0)

    def second_sweep(p, carry):
        def store(p, at, value):
            last[pl.ds(pl.multiple_of((p - SWEEPS) * rows + at, 8), size), :] = value

        sweep(state, p, store)
        return carry

    lax.fori_loop(SWEEPS, gx + SWEEPS, second_sweep, 0)
    last[gx * rows :] = jnp.zeros((last.shape[0] - gx * rows, TILE), f32)


def sample_weights(sz, g, points, lines, table, w_ref, wz_ref):
    cut = sz.qw // MXU_LANES * MXU_LANES
    heights = (iota((TILE, TILE), 0).astype(f32) - MIDDLE) * math.sqrt(square)
    line_weights(sz, g, points, lines, w_ref)
    oz = points[pl.ds(pl.multiple_of(g * GROUP, GROUP), GROUP), 2 * sz.qw :]
    right = height_factors(oz[:, :cut]) if cut else None
    rest = oz[:, cut:] * math.sqrt(square)
    yield
    for u in range(GROUP):
        if cut:
            exponents = dot(table[u * TILE : (u + 1) * TILE], right)
            wz_ref[u * TILE : (u + 1) * TILE, :cut] = jnp.exp2(exponents).astype(bf16)
        for t in range(cut, sz.qw, TILE):
            away = rest[u : u + 1, t - cut : t - cut + TILE] - heights
            value = jnp.exp2(norm_bits - away * away).astype(bf16)
            wz_ref[u * TILE : (u + 1) * TILE, t : t + TILE] = value
        yield


def weights_kernel(sz, parts, *refs):
    recv, (table, w_out, wz_out, points, lines) = refs[:parts], refs[parts:]
    load_records(sz, recv, points, lines)
    count = w_out.shape[0]
    turns = next(t for t in (4, 2, 1) if count % t == 0)

    def step(h, carry):
        groups = [turns * h + i for i in range(turns)]
        for g in groups:
            in_turn(sample_weights(sz, g, points, lines, table, w_out.at[g], wz_out.at[g]))
        return carry

    lax.fori_loop(0, count // turns, step, 0)


def sample_kernel(sz, gx, ny, nyb, layers, slabs, parts, begin, halves, *refs):
    lines_in, refs = refs[:parts], refs[parts:]
    if begin:
        ready, refs = refs[: 2 * halves], refs[2 * halves :]
        expand, own, other, last, vnew = refs[:5]
        back, (drive, state, *refs) = refs[5 : 5 + parts], refs[5 + parts :]
    else:
        recv, (expand, table, last), refs = refs[:parts], refs[parts : 3 + parts], refs[3 + parts :]
        back, (points, lines, w0, wz0, w1, wz1, *refs) = refs[:parts], refs[parts:]
    gathered, products, sampled, rows_s, sem = refs
    copies = []
    for i, part in enumerate(lines_in):
        size = part.shape[0]
        copies.append(pltpu.make_async_copy(part, rows_s.at[pl.ds(i * size, size)], sem.at[i]))
        copies[-1].start()
    stencil = sz.stencil
    slots = sampled.shape[0]
    count = slots // GROUP
    planes = 3 * layers
    if not begin:
        load_records(sz, recv, points, lines)
    else:
        relax(gx, ny, layers, slabs, own, other, drive, state, last)
        size = nyb * planes
        for x in range(gx):
            at = pl.multiple_of(x * ny * planes + lax.axis_index("batch") * size, 8)
            vnew[x * size : (x + 1) * size] = last[pl.ds(at, size), :]
    shape = (3 * GROUP, 3 * GROUP * stencil)
    cell, part = iota(shape, 1) // (3 * stencil), iota(shape, 1) // stencil % 3
    adds = one_hot(iota(shape, 0) == part * GROUP + cell)

    for copy in copies:
        copy.wait()
    def prepare(g, w_ref, wz_ref):
        yield from sample_weights(sz, jnp.minimum(g, count - 1), points, lines, table, w_ref, wz_ref)

    def use(g, w_ref, wz_ref):
        first = pl.multiple_of(g * GROUP, GROUP)
        for u in range(GROUP):
            for j in range(stencil):
                spot = pl.ds(rows_s[first + u, j], 3, stride=layers)
                gathered[u, 4 * j : 4 * j + 3] = last[spot, :]
        for u in range(GROUP):
            tiles = [
                gathered[u, pl.ds(4 * j + k, 8, stride=4), :] for k in range(3) for j in range(0, stencil, 8)
            ]
            projected = dot(jnp.concatenate(tiles, axis=0).astype(bf16), wz_ref[u * TILE : (u + 1) * TILE])
            w = w_ref[u * stencil : (u + 1) * stencil]
            for k in range(3):
                at = (u * 3 + k) * stencil
                products[at : at + stencil] = (projected[k * stencil : (k + 1) * stencil] * w).astype(bf16)
            yield
        values = dot(adds, products[...])
        for k in range(3):
            sampled[pl.ds(first, GROUP), k * sz.qw : (k + 1) * sz.qw] = values[k * GROUP : (k + 1) * GROUP]

    def use_ready(base, w_in, wz_in):
        turns = next(t for t in (UNROLL, 6, 4, 2, 1) if w_in.shape[0] % t == 0)

        def step(h, carry):
            for i in range(turns):
                g = turns * h + i
                in_turn(use(base + g, w_in.at[g], wz_in.at[g]))
            return carry

        lax.fori_loop(0, w_in.shape[0] // turns, step, 0)

    if begin:
        base = 0
        for w_in, wz_in in zip(ready[::2], ready[1::2]):
            use_ready(base, w_in, wz_in)
            base += w_in.shape[0]
    else:
        run_groups(count, prepare, use, ((w0, wz0), (w1, wz1)))
    coef = dot(sampled[...].astype(bf16), expand[...]).astype(bf16)
    base = 0
    for ref in back:
        ref[...] = coef[base : base + ref.shape[0]]
        base += ref.shape[0]


def unpack_kernel(sz, *refs):
    slot, out = refs[0], refs[-1]
    parts = refs[1:-1]
    back = jnp.concatenate([part[...] for part in parts], axis=0)
    place = one_hot(slot[...] == iota((back.shape[0], slot.shape[1]), 0))
    coef = dot(place, back, 0, 0)
    coef = coef.astype(bf16)
    for k in range(3):
        shape = (sz.terms, sz.cw)
        pick = one_hot(iota(shape, 1) == iota(shape, 0) + k * sz.terms)
        out[k] = dot(pick, coef, 1, 1).astype(bf16)


def local(
    velocity_old, traction, offsets, owner_slab, anchor, blocks, block_count, synthesis, analysis
):
    cells, _, terms = traction.shape
    gx, nyb, layers = velocity_old.shape[:3]
    slabs, batches = lax.axis_size("slab"), lax.axis_size("batch")
    ny = nyb * batches
    planes = 3 * layers
    cap = 2 * cells // slabs
    stencil = blocks.shape[1]
    sz = Sizes(terms, offsets.shape[2], stencil)
    half = ny // 2
    grid_rows = gx * ny * planes + 8 * planes

    pairwise = cap % 16 == 0 and slabs & (slabs - 1) == 0
    if pairwise:
        chunks, size = slabs, cap
        stages = [list(range(min(4, slabs)))] + ([list(range(4, slabs))] if slabs > 4 else [])
        back_stages = [list(range(4, slabs)), list(range(1, min(4, slabs))), [0]]
        back_stages = [stage for stage in back_stages if stage]
    else:
        chunks = next(c for c in (3, 2, 1) if cap % c == 0 and slabs * (cap // c) % 16 == 0)
        size = slabs * cap // chunks
        stages = back_stages = [[c] for c in range(chunks)]

    def exchange(value, p):
        if not pairwise:
            return lax.all_to_all(value, "slab", split_axis=0, concat_axis=0, tiled=True)
        return lax.ppermute(value, "slab", [(i, i ^ p) for i in range(slabs)]) if p else value

    def shape(dims, dtype):
        return jax.ShapeDtypeStruct(dims, dtype)

    def whole(dims):
        return pl.BlockSpec(dims, lambda i: (0,) * len(dims))

    packed = [
        owner_slab.T,
        anchor.T,
        blocks.T,
        block_count.reshape(1, cells),
        traction.transpose(1, 2, 0),
        offsets.transpose(1, 0, 2),
    ]
    send = pl.pallas_call(
        lambda *refs: pack_kernel(sz, slabs, cap, chunks, pairwise, ny, layers, *refs),
        grid=(1,),
        out_shape=[shape((size, sz.width), bf16)] * chunks + [shape((1, cells), jnp.int32)],
        in_specs=[whole(value.shape) for value in packed],
        out_specs=[whole((size, sz.width))] * chunks + [whole((1, cells))],
        scratch_shapes=[pltpu.VMEM((cells, sz.width), bf16)],
        compiler_params=pltpu.CompilerParams(vmem_limit_bytes=60 * 1024 * 1024),
        name="pack",
    )(*packed)
    slot = send[chunks]
    recv = [exchange(send[p], p) for p in range(chunks)]

    def basis(values, dim):
        table = (TILE, GROUP * TILE) if dim else (GROUP * TILE, TILE)
        return pl.pallas_call(
            lambda *refs: basis_kernel(sz, dim, *refs),
            out_shape=[shape((sz.cw, 3 * sz.qw) if dim else (3 * sz.qw, sz.cw), bf16), shape(table, bf16)],
            in_specs=vmem(1),
            out_specs=vmem(2),
            compiler_params=params,
            name="basis",
        )(values)

    spread_basis, spread_table = basis(synthesis, 1)

    grid_shape = shape((grid_rows, TILE), f32)
    half_shape = shape((gx * planes * half, TILE), bf16)
    weights_xy = pltpu.VMEM((GROUP * stencil, sz.qw), f32)
    terms_shape = pltpu.VMEM((GROUP, 4 * stencil, TILE), f32)
    grid = velocity_old.transpose(0, 1, 3, 2, 4).reshape(-1, TILE)
    rows = {}
    for stage in stages:
        parts = len(stage)
        slots = parts * size
        begin, end = stage is stages[0], stage is stages[-1]
        points = [pltpu.VMEM((slots, 3 * sz.qw), f32), pltpu.VMEM((2, slots // GROUP, TILE), f32)]
        out = pl.pallas_call(
            lambda *refs: spread_kernel(sz, gx, ny, nyb, layers, parts, begin, end, *refs),
            out_shape=[
                grid_shape,
            ]
            + [shape((size, TILE), jnp.int32)] * parts
            + [half_shape] * (2 * end),
            in_specs=vmem(parts + 3),
            out_specs=vmem(1 + parts + 2 * end),
            scratch_shapes=points
            + [pltpu.VMEM((slots, 3 * sz.qw), f32)]
            + [weights_xy, pltpu.VMEM((sz.qw, GROUP * TILE), bf16)] * 2
            + [terms_shape, pltpu.SMEM((slots, TILE), jnp.int32), pltpu.SemaphoreType.DMA((parts,))],
            input_output_aliases={} if begin else {2 + parts: 0},
            compiler_params=params,
            cost_estimate=pl.CostEstimate(flops=100_000_000 * slots, bytes_accessed=4_000_000, transcendentals=0),
            name="spread",
        )(*(recv[p] for p in stage), spread_basis, spread_table, grid)
        grid = out[0]
        rows.update(zip(stage, out[1 : 1 + parts]))
    keep, send_half = out[-2:]

    def pairs(bit):
        return [(i, i ^ bit) for i in range(batches)]

    def add(a, b):
        return (a.astype(f32) + b.astype(f32)).astype(bf16)

    mine = add(keep, lax.ppermute(send_half, "batch", pairs(1)))
    def weights(values):
        slots = len(values) * size
        groups = slots // GROUP
        return pl.pallas_call(
            lambda *refs: weights_kernel(sz, len(values), *refs),
            out_shape=[
                shape((groups, GROUP * stencil, sz.qw), f32),
                shape((groups, GROUP * TILE, sz.qw), bf16),
            ],
            in_specs=vmem(len(values) + 1),
            out_specs=vmem(2),
            scratch_shapes=[pltpu.VMEM((slots, 3 * sz.qw), f32), pltpu.VMEM((2, groups, TILE), f32)],
            compiler_params=params,
            cost_estimate=pl.CostEstimate(flops=50_000_000 * slots, bytes_accessed=4_000_000, transcendentals=0),
            name="weights",
        )(*values, sample_table)

    first = back_stages[0]
    late = [recv[p] for p in first]
    mine, analysis, late = lax.optimization_barrier((mine, analysis, late))
    sample_basis, sample_table = basis(analysis, 0)
    ready = [weights(late[: (len(late) + 1) // 2])]
    halo = SWEEPS * planes * half
    low = lax.ppermute(mine[-halo:], "slab", [(i, i + 1) for i in range(slabs - 1)])
    high = lax.ppermute(mine[:halo], "slab", [(i + 1, i) for i in range(slabs - 1)])
    edges = jnp.concatenate([low, high], axis=0)
    bit = 2
    while bit < batches:
        got = lax.ppermute(mine, "batch", pairs(bit))
        edges, got, ready, late = lax.optimization_barrier((edges, got, ready, late))
        mine = add(mine, got)
        edges = add(edges, lax.ppermute(edges, "batch", pairs(bit)))
        bit *= 2
    mine = jnp.concatenate([edges[:halo], mine, edges[halo:]], axis=0)
    if len(late) > 1:
        ready.append(weights(late[(len(late) + 1) // 2 :]))
        mine, ready = lax.optimization_barrier((mine, ready))
    other = lax.ppermute(mine, "batch", pairs(1))

    wide = gx + 2 * SWEEPS
    padded = pltpu.VMEM((wide, planes * ny + 16, TILE), f32)
    returned = [None] * chunks
    for stage in back_stages:
        parts = len(stage)
        slots = parts * size
        begin = stage is back_stages[0]
        out = pl.pallas_call(
            lambda *refs: sample_kernel(sz, gx, ny, nyb, layers, slabs, parts, begin, len(ready), *refs),
            out_shape=([grid_shape, shape((gx * nyb * planes, TILE), f32)] if begin else [])
            + [shape((size, sz.cw), bf16)] * parts,
            in_specs=vmem(parts + 2 * len(ready) + 3 if begin else 2 * parts + 3),
            out_specs=vmem(2 * begin + parts),
            scratch_shapes=(
                [padded, padded]
                if begin
                else [pltpu.VMEM((slots, 3 * sz.qw), f32), pltpu.VMEM((2, slots // GROUP, TILE), f32)]
                + [weights_xy, pltpu.VMEM((GROUP * TILE, sz.qw), bf16)] * 2
            )
            + [terms_shape]
            + [pltpu.VMEM((3 * GROUP * stencil, sz.qw), bf16), pltpu.VMEM((slots, 3 * sz.qw), f32)]
            + [pltpu.SMEM((slots, TILE), jnp.int32), pltpu.SemaphoreType.DMA((parts,))],
            compiler_params=params,
            cost_estimate=pl.CostEstimate(flops=50_000_000 * slots, bytes_accessed=4_000_000, transcendentals=0),
            name="sample",
        )(
            *(rows[p] for p in stage),
            *((*sum(map(list, ready), []), sample_basis, mine, other) if begin else (*(recv[p] for p in stage), sample_basis, sample_table, grid)),
        )
        if begin:
            grid, vnew = out[:2]
        for p, back in zip(stage, out[2 * begin :]):
            returned[p] = exchange(back, p)
    velocity_new = vnew.reshape(gx, nyb, 3, layers, TILE).transpose(0, 1, 3, 2, 4)

    coef = pl.pallas_call(
        lambda *refs: unpack_kernel(sz, *refs),
        out_shape=shape((3, terms, cells), bf16),
        in_specs=vmem(1 + chunks),
        out_specs=vmem(1)[0],
        compiler_params=params,
        name="unpack",
    )(slot, *returned)
    return velocity_new, coef.transpose(2, 0, 1)


def solution(mesh):
    in_specs = (
        P("slab", "batch", None, None, None),
        P(("slab", "batch"), None, None),
        P(("slab", "batch"), None, None),
        P(("slab", "batch"), None),
        P(("slab", "batch"), None),
        P(("slab", "batch"), None),
        P(("slab", "batch")),
        P(),
        P(),
    )
    out_specs = (P("slab", "batch", None, None, None), P(("slab", "batch"), None, None))
    return jax.shard_map(local, mesh=mesh, in_specs=in_specs, out_specs=out_specs, check_vma=False)
```
